128 devices in a mesh: row: 4 (over x), col: 16 (over z, y_lo, core), depth: 2 (over y_hi).
Axes of the slice: x: 4, y: 4 (y_hi: 2, y_lo: 2; y = y_hi * 2 + y_lo), z: 4, core: 2. Of those that a mesh axis runs over, the one named last changes fastest.
Arguments:
- tokens: bfloat16 [1024, 7168], P(('col', 'depth'), 'row'), may hold values from -6 to 6
- first_weight: bfloat16 [7168, 28672], P('row', 'col'), may hold values from -0.0625 to 0.0625
- second_weight: bfloat16 [28672, 7168], P('col', 'row'), may hold values from -0.03125 to 0.03125
- upstream: bfloat16 [1024, 7168], P(('col', 'depth'), 'row'), may hold values from -6 to 6
Outputs:
- layer_out: bfloat16 [1024, 7168], P(('col', 'depth'), 'row')
- token_grad: bfloat16 [1024, 7168], P(('col', 'depth'), 'row')
- first_grad: float32 [7168, 28672], P(('row', 'depth'), 'col')
- second_grad: float32 [28672, 7168], P(('col', 'depth'), 'row')
The draws below stay inside these ranges and needn't reach their ends.
All inputs are finite; a program needn't handle non-finite values.
Results may differ from the reference program's by a relative error of at most 0.005.
Values may be sent and summed in bfloat16 or wider, within the bound.
A program may use at most 192 MiB of HBM per device.

```python
import math
import jax
import jax.numpy as jnp

D = 7168
FF = 28672
TOKENS = 1024


def block_scale(own_key, shape, cuts, least, high):
    level, own = 1.0, jax.random.fold_in(own_key, 6)
    for position, blocks in cuts:
        steps = jnp.exp(jax.random.uniform(jax.random.fold_in(own, position), (blocks,), jnp.float32, least / len(cuts), high / len(cuts)))
        level = level * jnp.repeat(steps, shape[position] // blocks).reshape([-1 if axis == position else 1 for axis in range(len(shape))])
    return level


def gaussian(rng, shape, spread, limit, pieces=(), kind=jnp.bfloat16):
    result = jax.random.normal(rng, shape, jnp.float32) * spread
    if len(pieces) > 0:
        result = block_scale(rng, shape, pieces, -0.22, 0.18) * result
    return jnp.clip(result, min=-limit, max=limit).astype(kind)


def setup_inputs(seed: int = 0) -> dict:
    arg_keys = jax.random.split(jax.random.key(seed), 5)
    return {
        "tokens": gaussian(arg_keys[0], (TOKENS, D), 1.0, 6.0, ((0, 32), (1, 4))),
        "first_weight": gaussian(arg_keys[1], (D, FF), D ** -0.5, 0.0625, ((0, 4), (1, 16))),
        "second_weight": gaussian(arg_keys[2], (FF, D), FF ** -0.5, 0.03125, ((0, 16), (1, 4))),
        "upstream": gaussian(arg_keys[3], (TOKENS, D), 1.0, 6.0, ((0, 32), (1, 4))),
    }


def gelu_tanh(hidden):
    scale = math.sqrt(2.0 / math.pi)
    inner = scale * (hidden + 0.044715 * hidden * hidden * hidden)
    return 0.5 * hidden * (1.0 + jnp.tanh(inner))

def gelu_slope(hidden):
    scale = math.sqrt(2.0 / math.pi)
    inner = scale * (hidden + 0.044715 * hidden * hidden * hidden)
    tanh_val = jnp.tanh(inner)
    return 0.5 * (1.0 + tanh_val) + 0.5 * hidden * (1.0 - tanh_val * tanh_val) * scale * (1.0 + 3.0 * 0.044715 * hidden * hidden)

def reference(tokens, first_weight, second_weight, upstream):
    hidden = jnp.dot(tokens, first_weight, preferred_element_type=jnp.float32)
    activ = gelu_tanh(hidden).astype(jnp.bfloat16)
    layer_out = jnp.dot(activ, second_weight, preferred_element_type=jnp.float32).astype(jnp.bfloat16)
    back_hidden = jnp.dot(upstream, second_weight.T, preferred_element_type=jnp.float32)
    delta = (back_hidden * gelu_slope(hidden)).astype(jnp.bfloat16)
    token_grad = jnp.dot(delta, first_weight.T, preferred_element_type=jnp.float32).astype(jnp.bfloat16)
    first_grad = jnp.dot(tokens.T, delta, preferred_element_type=jnp.float32)
    second_grad = jnp.dot(activ.T, upstream, preferred_element_type=jnp.float32)
    return (layer_out, token_grad, first_grad, second_grad)
```

```python
import functools
import math

import jax
import jax.numpy as jnp
from jax import lax
from jax.experimental import pallas as pl
from jax.experimental.pallas import tpu as pltpu
from jax.sharding import PartitionSpec as P

MESH = pl.DeviceIdType.MESH
BF = jnp.bfloat16
F32 = jnp.float32
SCALE = math.sqrt(2.0 / math.pi)

W = 1792
H = 896
C = 256
Q = 64
B = 32
UNITS = ((0, 0), (0, 1), (1, 1), (0, 2), (1, 2), (0, 3), (1, 3), (1, 0))
OFFSET = (0, 1, 3, 2)


def gelu_and_slope(h):
    inner = SCALE * (h + 0.044715 * h * h * h)
    t = jnp.tanh(inner)
    value = 0.5 * h * (1.0 + t)
    slope = 0.5 * (1.0 + t) + 0.5 * h * (1.0 - t * t) * SCALE * (
        1.0 + 3.0 * 0.044715 * h * h
    )
    return value, slope


def kernel(
    tok_ref, w1_ref, w2_ref, up_ref,
    lo_ref, tg_ref, fg_ref, sg_ref,
    xs, wa, wb, hp, rs1s, rs1r, rs2s, rs2r, agb, slope, pdelta,
    keep, sibs, sibr, zs, zr, s0, ys, yr, facc,
    lsem, gsend, grecv, usend, urecv, fsend, frecv,
):
    x = lax.axis_index("row")
    col = lax.axis_index("col")
    yh = lax.axis_index("depth")
    z, yl, c = col // 4, (col // 2) % 2, col % 2
    y = yh * 2 + yl

    def dev(dx=0, dy=0, dz=0, dc=0):
        xx, yy = lax.rem(x + dx, 4), lax.rem(y + dy, 4)
        zz, cc = lax.rem(z + dz, 4), lax.rem(c + dc, 2)
        return (xx, zz * 4 + lax.rem(yy, 2) * 2 + cc, yy // 2)

    pending, waited = [], []

    def send(src, dst, ss, rs, to):
        cp = pltpu.make_async_remote_copy(
            src_ref=src, dst_ref=dst, send_sem=ss, recv_sem=rs,
            device_id=to, device_id_type=MESH,
        )
        cp.start()
        pending.append(cp)
        return cp

    def rows(start, size):
        return pl.ds(pl.multiple_of(start, size), size)

    half = rows(yh * H, H)
    in_copies = [
        pltpu.make_async_copy(tok_ref, xs.at[0, z, rows(c * 128 + y * B, B)], lsem.at[0]),
        pltpu.make_async_copy(up_ref, xs.at[1, z, rows(c * 128 + y * B, B)], lsem.at[1]),
        pltpu.make_async_copy(w1_ref.at[:, half], wa.at[0], lsem.at[2]),
        pltpu.make_async_copy(w2_ref.at[half, :], wb.at[0], lsem.at[3]),
    ]
    for cp in in_copies:
        cp.start()

    barrier = pltpu.get_barrier_semaphore()
    peers = [dev(dc=1), dev(dx=1), dev(dx=3), dev(dy=1), dev(dy=2), dev(dy=3),
             dev(dz=1), dev(dz=2), dev(dz=3)]
    for p in peers:
        pl.semaphore_signal(barrier, inc=1, device_id=p, device_id_type=MESH)
    pl.semaphore_wait(barrier, len(peers))

    G = {}

    def gsem(k, i):
        return gsend.at[k, i], grecv.at[k, i]

    def gather_y(k):
        in_copies[k].wait()
        blk = xs.at[k, z, rows(c * 128 + y * B, B)]
        for d in (1, 3, 2):
            G[k, "y", d] = send(blk, blk, *gsem(k, d - 1), dev(dy=d))

    def gather_z(k):
        for d in (1, 3, 2):
            G[k, "y", d].wait_recv()
        grp = xs.at[k, z, rows(c * 128, 128)]
        G[k, "s", 0] = send(grp, grp, *gsem(k, 3), dev(dc=1))
        G[k, "z", 1] = send(grp, grp, *gsem(k, 4), dev(dz=1))
        G[k, "z", 3] = send(grp, grp, *gsem(k, 5), dev(dz=3))

    def gather_relay(k, chunk):
        zz = lax.rem(z + OFFSET[chunk], 4)
        G[k, "z", 3 if chunk == 1 else 1].wait_recv()
        if chunk == 1:
            part = xs.at[k, zz, rows(c * 128 + 64, 64)]
            G[k, "r", 1] = send(part, part, *gsem(k, 6), dev(dz=3))
        else:
            part = xs.at[k, zz, rows(c * 128, 64)]
            G[k, "r", 2] = send(part, part, *gsem(k, 7), dev(dz=1))
        grp = xs.at[k, zz, rows(c * 128, 128)]
        G[k, "s", chunk] = send(grp, grp, *gsem(k, 7 + chunk), dev(dc=1))

    def gather_last(k):
        G[k, "r", 1].wait_recv()
        G[k, "r", 2].wait_recv()
        grp = xs.at[k, lax.rem(z + 2, 4), rows(c * 128, 128)]
        G[k, "s", 3] = send(grp, grp, *gsem(k, 10), dev(dc=1))

    def gather_done(k, chunk):
        G[k, "s", chunk].wait_recv()

    U = {}

    def usem(u, i):
        return usend.at[u, i], urecv.at[u, i]

    def stage_a(u):
        kind, chunk = UNITS[u]
        zz = lax.rem(z + OFFSET[chunk], 4)
        slot = u % 3

        def tile(n, width):
            at = pl.ds(n, width)
            hp[slot, :, at] = jnp.dot(
                xs[kind, zz], wa[kind, :, at], preferred_element_type=F32
            )

        @pl.loop(0, 3)
        def _(i):
            tile(pl.multiple_of(i * 256, 256), 256)

        tile(768, 128)
        rs1s[u] = hp[slot, rows(lax.rem(x + 2, 4) * Q, Q)].astype(BF)
        U[u, "a", 0] = send(rs1s.at[u, 0:32], rs1r.at[u, 0], *usem(u, 0), dev(dx=1))
        U[u, "a", 1] = send(rs1s.at[u, 32:64], rs1r.at[u, 1], *usem(u, 1), dev(dx=3))

    def stage_b(u):
        slot = u % 3
        to_right = lax.rem(x + 1, 4) * Q
        to_left = lax.rem(x + 3, 4) * Q
        U[u, "a", 0].wait_recv()
        rs2s[u, 0, 0:32] = (hp[slot, rows(to_right, 32)] + rs1r[u, 0].astype(F32)).astype(BF)
        rs2s[u, 0, 32:64] = hp[slot, rows(to_right + 32, 32)].astype(BF)
        U[u, "b", 0] = send(rs2s.at[u, 0], rs2r.at[u, 0], *usem(u, 2), dev(dx=1))
        U[u, "a", 1].wait_recv()
        rs2s[u, 1, 0:32] = hp[slot, rows(to_left, 32)].astype(BF)
        rs2s[u, 1, 32:64] = (hp[slot, rows(to_left + 32, 32)] + rs1r[u, 1].astype(F32)).astype(BF)
        U[u, "b", 1] = send(rs2s.at[u, 1], rs2r.at[u, 1], *usem(u, 3), dev(dx=3))

    def stage_c(u):
        kind, chunk = UNITS[u]
        slot = u % 3
        U[u, "b", 0].wait_recv()
        U[u, "b", 1].wait_recv()
        for r in range(0, Q, 32):
            h = hp[slot, rows(x * Q + r, 32)]
            h = h + rs2r[u, 0, r : r + 32].astype(F32) + rs2r[u, 1, r : r + 32].astype(F32)
            if kind == 0:
                value, sl = gelu_and_slope(h)
                slope[chunk, r : r + 32] = sl
            else:
                value = h * slope[chunk, r : r + 32]
            agb[u, rows(x * Q + r, 32)] = value.astype(BF)
        mine = agb.at[u, rows(x * Q, Q)]
        U[u, "c", 0] = send(mine, mine, *usem(u, 4), dev(dx=1))
        U[u, "c", 1] = send(mine, mine, *usem(u, 5), dev(dx=3))

    def stage_d(u):
        U[u, "c", 0].wait_recv()
        part = agb.at[u, rows(lax.rem(x + 3, 4) * Q, 32)]
        U[u, "d", 0] = send(part, part, *usem(u, 6), dev(dx=1))
        U[u, "c", 1].wait_recv()
        part = agb.at[u, rows(lax.rem(x + 1, 4) * Q + 32, 32)]
        U[u, "d", 1] = send(part, part, *usem(u, 7), dev(dx=3))

    def stage_e(u):
        kind, chunk = UNITS[u]
        U[u, "d", 0].wait_recv()
        U[u, "d", 1].wait_recv()
        if kind == 1:
            U[u, "p"] = send(agb.at[u], pdelta.at[chunk], *usem(u, 8), dev(dy=2))
        away, own = rows((1 - c) * 128, 128), rows(c * 128, 128)
        if u >= 4:
            U[u - 4, "e"].wait_send()
            waited.append(id(U[u - 4, "e"]))

        @pl.loop(0, W // 256)
        def _(i):
            at = pl.ds(pl.multiple_of(i * 256, 256), 256)
            lhs = jnp.concatenate([agb[u, away], agb[u, own]], axis=0)
            part = jnp.dot(lhs, wb[kind, :, at], preferred_element_type=F32)
            sibs[u % 4, :, at] = part[:128].astype(BF)
            keep[u % 2, :, at] = part[128:]

        U[u, "e"] = send(sibs.at[u % 4], sibr.at[u], *usem(u, 9), dev(dc=1))

    def stage_f(u):
        kind, chunk = UNITS[u]
        U[u, "e"].wait_recv()

        @pl.loop(0, 4)
        def _(i):
            r = rows(i * 32, 32)
            total = keep[u % 2, r] + sibr[u, r].astype(F32)
            if chunk == 0:
                s0[kind, r] = total
            else:
                zs[kind, chunk - 1, r] = total.astype(BF)

        if chunk != 0:
            U[kind, chunk, "z"] = send(
                zs.at[kind, chunk - 1], zr.at[kind, chunk - 1], *usem(u, 10),
                dev(dz=OFFSET[chunk]),
            )

    def stage_g(kind):
        for chunk in (1, 2, 3):
            U[kind, chunk, "z"].wait_recv()

        def total(blk):
            r = rows(blk * B, B)
            t = s0[kind, r]
            for i in range(3):
                t = t + zr[kind, i, r].astype(F32)
            return t

        for d in (1, 3, 2):
            ys[kind, d] = total(lax.rem(y + d, 4)).astype(BF)
            U[kind, d, "y"] = send(
                ys.at[kind, d], yr.at[kind, d - 1], fsend.at[kind, d - 1],
                frecv.at[kind, d - 1], dev(dy=d),
            )
        s0[kind, 0:B] = total(y)

    def stage_h(kind):
        t = s0[kind, 0:B]
        for d in (1, 3, 2):
            U[kind, d, "y"].wait_recv()
            t = t + yr[kind, d - 1].astype(F32)
        (lo_ref, tg_ref)[kind][...] = t.astype(BF)

    def lead(a, b):
        return lax.dot_general(a, b, (((0,), (0,)), ((), ())), preferred_element_type=F32)

    acts = [UNITS.index((0, j)) for j in range(4)]

    def second_grad():
        @pl.loop(0, W // 256)
        def _(i):
            at = pl.ds(pl.multiple_of(i * 256, 256), 256)
            t = None
            for j in range(4):
                p = lead(agb[acts[j]], xs[1, lax.rem(z + OFFSET[j], 4), :, at])
                t = p if t is None else t + p
            wb[0, :, at] = t.astype(BF)

        cp = pltpu.make_async_copy(wb.at[0], sg_ref, lsem.at[4])
        cp.start()
        return cp

    def first_grad(chunk, own, first, last):
        src = agb.at[UNITS.index((1, chunk))] if own else pdelta.at[chunk]
        side = 0 if own else 1
        zz = lax.rem(z + OFFSET[chunk], 4)

        def tile(n, width):
            at = pl.ds(n, width)
            p = lead(xs[0, zz, :, half], src[:, at])
            if not first:
                p = p + facc[side, :, at]
            if last:
                wa[0, side * H : side * H + H, at] = p.astype(BF)
            else:
                facc[side, :, at] = p

        @pl.loop(0, 3)
        def _(i):
            tile(pl.multiple_of(i * 256, 256), 256)

        tile(768, 128)
        if last:
            to = rows((yh if own else 1 - yh) * H, H)
            cp = pltpu.make_async_copy(
                wa.at[0, side * H : side * H + H], fg_ref.at[:, to], lsem.at[5 + side]
            )
            cp.start()
            return cp

    gather_y(0)
    gather_y(1)
    in_copies[3].wait()

    @pl.loop(0, W // 256)
    def _(i):
        at = pl.ds(pl.multiple_of(i * 256, 256), 256)
        wa[1, at, :] = wb[0, :, at].T

    gather_z(0)
    gather_z(1)
    in_copies[2].wait()

    @pl.loop(0, W // 256)
    def _(i):
        at = pl.ds(pl.multiple_of(i * 256, 256), 256)
        wb[1, :, at] = wa[0, at, :].T

    gather_done(0, 0)
    stage_a(0)
    stage_b(0)
    stage_c(0)
    stage_d(0)
    gather_done(1, 0)
    gather_relay(0, 1)
    gather_relay(0, 2)
    gather_done(0, 1)
    stage_a(1)
    stage_e(0)
    stage_b(1)
    gather_relay(1, 1)
    gather_relay(1, 2)
    gather_done(1, 1)
    stage_a(2)
    stage_f(0)
    stage_c(1)
    stage_b(2)
    gather_last(0)
    gather_done(0, 2)
    stage_a(3)
    stage_d(1)
    stage_c(2)
    stage_b(3)
    stage_e(1)
    gather_last(1)
    gather_done(1, 2)
    stage_a(4)
    stage_d(2)
    stage_c(3)
    stage_b(4)
    stage_f(1)
    stage_e(2)
    gather_done(0, 3)
    stage_a(5)
    stage_d(3)
    stage_c(4)
    stage_b(5)
    stage_f(2)
    stage_e(3)
    gather_done(1, 3)
    stage_a(6)
    stage_d(4)
    stage_c(5)
    stage_b(6)
    stage_f(3)
    stage_e(4)
    first_grad(1, True, True, False)
    stage_a(7)
    stage_d(5)
    stage_c(6)
    stage_b(7)
    stage_f(4)
    stage_e(5)
    first_grad(2, True, False, False)
    U[2, "p"].wait_recv()
    first_grad(1, False, True, False)
    stage_d(6)
    stage_c(7)
    stage_f(5)
    stage_e(6)
    out = [second_grad()]
    stage_d(7)
    stage_f(6)
    stage_e(7)
    first_grad(3, True, False, False)
    stage_g(0)
    stage_f(7)
    stage_g(1)
    U[4, "p"].wait_recv()
    first_grad(2, False, False, False)
    out.append(first_grad(0, True, False, True))
    stage_h(0)
    U[6, "p"].wait_recv()
    first_grad(3, False, False, False)
    stage_h(1)
    U[7, "p"].wait_recv()
    out.append(first_grad(0, False, False, True))
    for cp in pending:
        if id(cp) not in waited:
            cp.wait_send()
    for cp in out:
        cp.wait()


def local(tokens, first_weight, second_weight, upstream):
    vm = pl.BlockSpec(memory_space=pltpu.VMEM)
    hbm = pl.BlockSpec(memory_space=pl.ANY)
    dma = pltpu.SemaphoreType.DMA
    lo, tg, fg, sg = pl.pallas_call(
        kernel,
        out_shape=(
            jax.ShapeDtypeStruct((B, W), BF),
            jax.ShapeDtypeStruct((B, W), BF),
            jax.ShapeDtypeStruct((H, W), BF),
            jax.ShapeDtypeStruct((H, W), BF),
        ),
        in_specs=[hbm] * 4,
        out_specs=(vm, vm, hbm, hbm),
        scratch_shapes=[
            pltpu.VMEM((2, 4, C, W), BF),
            pltpu.VMEM((2, W, H), BF),
            pltpu.VMEM((2, H, W), BF),
            pltpu.VMEM((3, C, H), F32),
            pltpu.VMEM((8, Q, H), BF),
            pltpu.VMEM((8, 2, 32, H), BF),
            pltpu.VMEM((8, 2, Q, H), BF),
            pltpu.VMEM((8, 2, Q, H), BF),
            pltpu.VMEM((8, C, H), BF),
            pltpu.VMEM((4, Q, H), F32),
            pltpu.VMEM((4, C, H), BF),
            pltpu.VMEM((2, 128, W), F32),
            pltpu.VMEM((4, 128, W), BF),
            pltpu.VMEM((8, 128, W), BF),
            pltpu.VMEM((2, 3, 128, W), BF),
            pltpu.VMEM((2, 3, 128, W), BF),
            pltpu.VMEM((2, 128, W), F32),
            pltpu.VMEM((2, 4, B, W), BF),
            pltpu.VMEM((2, 3, B, W), BF),
            pltpu.VMEM((2, H, H), F32),
            dma((7,)),
            dma((2, 11)), dma((2, 11)),
            dma((8, 11)), dma((8, 11)),
            dma((2, 3)), dma((2, 3)),
        ],
        compiler_params=pltpu.CompilerParams(
            collective_id=0, has_side_effects=True, vmem_limit_bytes=60 << 20
        ),
        cost_estimate=pl.CostEstimate(
            flops=6 * 2 * 1024 * W * H, bytes_accessed=16 << 20, transcendentals=0
        ),
        name="ffn",
    )(tokens, first_weight, second_weight, upstream)
    return lo, tg, fg.astype(F32), sg.astype(F32)


def solution(mesh):
    in_specs = (
        P(("col", "depth"), "row"),
        P("row", "col"),
        P("col", "row"),
        P(("col", "depth"), "row"),
    )
    out_specs = (
        P(("col", "depth"), "row"),
        P(("col", "depth"), "row"),
        P(("row", "depth"), "col"),
        P(("col", "depth"), "row"),
    )
    return jax.shard_map(local, mesh=mesh, in_specs=in_specs, out_specs=out_specs, check_vma=False)
```

```python
import math

import jax
import jax.numpy as jnp
from jax import lax
from jax.experimental import pallas as pl
from jax.experimental.pallas import tpu as pltpu
from jax.sharding import PartitionSpec as P

MESH = pl.DeviceIdType.MESH
BF = jnp.bfloat16
F32 = jnp.float32
SCALE = math.sqrt(2.0 / math.pi)

W = 1792
H = 896
C = 256
Q = 64
B = 32
OFFSET = (0, 1, 3, 2)
DIRECT_SUM = ((0, 0), (1, 0))
DIRECT_GATHER = ((1, 0), (1, 1))
DIRECT_Z = ()
FS, KS, SS = 3, 4, 4
RELAY_Z = (0, 1)
F1 = (0, 1, 2)

SCHEDULE = (
    ("gy", 0), ("gy", 1), ("gz", 0), ("a", 0, 0), ("gr", 0, 2), ("gr", 0, 1), ("c", 0, 0),
    ("gz", 1), ("a", 0, 2), ("a", 0, 1), ("d", 0, 0), ("gl", 0), ("b", 0, 2), ("a", 0, 3),
    ("b", 0, 1), ("b", 0, 3), ("t1",), ("c", 0, 2), ("t2",), ("gr", 1, 1), ("gr", 1, 2),
    ("c", 0, 3), ("c", 0, 1), ("a", 1, 1), ("d", 0, 3), ("gl", 1), ("a", 1, 2), ("a", 1, 3),
    ("d", 0, 2), ("e", 0, 3), ("d", 0, 1), ("b", 1, 3), ("b", 1, 2), ("f", 0, 3), ("e", 0, 2),
    ("e", 0, 1), ("c", 1, 3), ("b", 1, 1), ("e", 0, 0), ("f", 0, 1), ("f", 0, 2), ("d", 1, 3),
    ("c", 1, 2), ("c", 1, 1), ("p", 1, 3), ("e", 1, 3), ("d", 1, 2), ("a", 1, 0), ("f", 1, 3),
    ("f", 0, 0), ("sg", 0), ("e", 1, 1), ("e", 1, 2), ("f1s", 1, 2), ("f", 1, 1), ("f", 1, 2),
    ("c", 1, 0), ("fo", 3), ("sg", 1), ("f1r", 1, 2), ("f1s", 1, 0), ("g", 0), ("f1s", 1, 1),
    ("e", 1, 0), ("fo", 1), ("f", 1, 0), ("g", 1), ("fp", 2), ("fo", 2), ("fp", 0), ("fo", 0),
    ("fp", 3), ("fp", 1), ("h", 0), ("h", 1),
)


def gelu_and_slope(h):
    inner = SCALE * (h + 0.044715 * h * h * h)
    t = jnp.tanh(inner)
    value = 0.5 * h * (1.0 + t)
    slope = 0.5 * (1.0 + t) + 0.5 * h * (1.0 - t * t) * SCALE * (
        1.0 + 3.0 * 0.044715 * h * h
    )
    return value, slope


def kernel(
    tok_ref, w1_ref, w2_ref, up_ref,
    lo_ref, tg_ref, fg_ref, sg_ref,
    xs, wa, wb, hp, rs1s, rs1r, rs2s, rs2r, agb, slope, pdelta,
    keep, sibs, sibr, zs, zr, s0, ys, yr, facc,
    lsem, gsend, grecv, usend, urecv, fsend, frecv,
):
    x = lax.axis_index("row")
    col = lax.axis_index("col")
    yh = lax.axis_index("depth")
    z, yl, c = col // 4, (col // 2) % 2, col % 2
    y = yh * 2 + yl

    def dev(dx=0, dy=0, dz=0, dc=0):
        xx, yy = lax.rem(x + dx, 4), lax.rem(y + dy, 4)
        zz, cc = lax.rem(z + dz, 4), lax.rem(c + dc, 2)
        return (xx, zz * 4 + lax.rem(yy, 2) * 2 + cc, yy // 2)

    pending, waited = [], []

    def send(src, dst, ss, rs, to):
        cp = pltpu.make_async_remote_copy(
            src_ref=src, dst_ref=dst, send_sem=ss, recv_sem=rs,
            device_id=to, device_id_type=MESH,
        )
        cp.start()
        pending.append(cp)
        return cp

    def rows(start, size):
        return pl.ds(pl.multiple_of(start, size), size)

    half = rows(yh * H, H)
    in_copies = [
        pltpu.make_async_copy(tok_ref, xs.at[0, z, rows(c * 128 + y * B, B)], lsem.at[0]),
        pltpu.make_async_copy(up_ref, xs.at[1, z, rows(c * 128 + y * B, B)], lsem.at[1]),
        pltpu.make_async_copy(w1_ref.at[:, half], wa.at[0], lsem.at[2]),
        pltpu.make_async_copy(w2_ref.at[half, :], wb.at[0], lsem.at[3]),
    ]
    for cp in in_copies:
        cp.start()
    loaded = set()

    def ready(i):
        if i not in loaded:
            loaded.add(i)
            in_copies[i].wait()

    barrier = pltpu.get_barrier_semaphore()
    peers = [dev(dc=1), dev(dx=1), dev(dx=2), dev(dx=3), dev(dy=1), dev(dy=2), dev(dy=3),
             dev(dz=1), dev(dz=2), dev(dz=3)]
    for p in peers:
        pl.semaphore_signal(barrier, inc=1, device_id=p, device_id_type=MESH)
    pl.semaphore_wait(barrier, len(peers))

    G = {}

    def gsem(k, i):
        return gsend.at[k, i], grecv.at[k, i]

    def gather_y(k):
        ready(k)
        blk = xs.at[k, z, rows(c * 128 + y * B, B)]
        for d in (1, 3, 2):
            G[k, "y", d] = send(blk, blk, *gsem(k, d - 1), dev(dy=d))

    def gather_z(k):
        for d in (1, 3, 2):
            G[k, "y", d].wait_recv()
        grp = xs.at[k, z, rows(c * 128, 128)]
        G[k, "s", 0] = send(grp, grp, *gsem(k, 3), dev(dc=1))
        G[k, "z", 1] = send(grp, grp, *gsem(k, 4), dev(dz=1))
        G[k, "z", 3] = send(grp, grp, *gsem(k, 5), dev(dz=3))
        if k in DIRECT_Z:
            G[k, "r", 1] = send(grp, grp, *gsem(k, 6), dev(dz=2))

    def gather_relay(k, chunk):
        zz = lax.rem(z + OFFSET[chunk], 4)
        G[k, "z", 3 if chunk == 1 else 1].wait_recv()
        if k in DIRECT_Z:
            pass
        elif chunk == 1:
            part = xs.at[k, zz, rows(c * 128 + 64, 64)]
            G[k, "r", 1] = send(part, part, *gsem(k, 6), dev(dz=3))
        else:
            part = xs.at[k, zz, rows(c * 128, 64)]
            G[k, "r", 2] = send(part, part, *gsem(k, 7), dev(dz=1))
        grp = xs.at[k, zz, rows(c * 128, 128)]
        G[k, "s", chunk] = send(grp, grp, *gsem(k, 7 + chunk), dev(dc=1))

    def gather_last(k):
        G[k, "r", 1].wait_recv()
        if k not in DIRECT_Z:
            G[k, "r", 2].wait_recv()
        grp = xs.at[k, lax.rem(z + 2, 4), rows(c * 128, 128)]
        G[k, "s", 3] = send(grp, grp, *gsem(k, 10), dev(dc=1))

    grouped = set()

    def group(k, chunk):
        if (k, chunk) not in grouped:
            grouped.add((k, chunk))
            G[k, "s", chunk].wait_recv()

    U = {}
    free_f, free_k, sib_sends = list(range(FS)), list(range(KS)), []
    slot_f, slot_k = {}, {}

    def usem(u, i):
        n = u[0] * 4 + u[1]
        return usend.at[n, i], urecv.at[n, i]

    def buf(ref, u):
        return ref.at[u[0] * 4 + u[1]]

    def stage_a(*u):
        kind, chunk = u
        group(kind, chunk)
        if kind == 0:
            ready(2)
        zz = lax.rem(z + OFFSET[chunk], 4)
        f = hp.at[slot_f.setdefault(u, free_f.pop(0))]
        f[...] = jnp.dot(xs[kind, zz], wa[kind], preferred_element_type=F32)
        away, into = buf(rs1s, u), buf(rs1r, u)
        away[...] = f[rows(lax.rem(x + 2, 4) * Q, Q)].astype(BF)
        if u in DIRECT_SUM:
            U[u, "a", 0] = send(away, into, *usem(u, 0), dev(dx=2))
            out, into = buf(rs2s, u), buf(rs2r, u)
            out[0] = f[rows(lax.rem(x + 1, 4) * Q, Q)].astype(BF)
            U[u, "b", 0] = send(out.at[0], into.at[0], *usem(u, 2), dev(dx=1))
            out[1] = f[rows(lax.rem(x + 3, 4) * Q, Q)].astype(BF)
            U[u, "b", 1] = send(out.at[1], into.at[1], *usem(u, 3), dev(dx=3))
            return
        U[u, "a", 0] = send(away.at[0:32], into.at[0:32], *usem(u, 0), dev(dx=1))
        U[u, "a", 1] = send(away.at[32:64], into.at[32:64], *usem(u, 1), dev(dx=3))

    def stage_b(*u):
        f = hp.at[slot_f[u]]
        right, left = lax.rem(x + 1, 4) * Q, lax.rem(x + 3, 4) * Q
        out, got, into = buf(rs2s, u), buf(rs1r, u), buf(rs2r, u)
        U[u, "a", 0].wait_recv()
        out[0, 0:32] = (f[rows(right, 32)] + got[0:32].astype(F32)).astype(BF)
        out[0, 32:64] = f[rows(right + 32, 32)].astype(BF)
        U[u, "b", 0] = send(out.at[0], into.at[0], *usem(u, 2), dev(dx=1))
        U[u, "a", 1].wait_recv()
        out[1, 0:32] = f[rows(left, 32)].astype(BF)
        out[1, 32:64] = (f[rows(left + 32, 32)] + got[32:64].astype(F32)).astype(BF)
        U[u, "b", 1] = send(out.at[1], into.at[1], *usem(u, 3), dev(dx=3))

    def stage_c(*u):
        kind, chunk = u
        f, got, ag = hp.at[slot_f[u]], buf(rs2r, u), buf(agb, u)
        U[u, "b", 0].wait_recv()
        U[u, "b", 1].wait_recv()
        if u in DIRECT_SUM:
            U[u, "a", 0].wait_recv()
        for r in range(0, Q, 32):
            h = f[rows(x * Q + r, 32)]
            h = h + got[0, r : r + 32].astype(F32) + got[1, r : r + 32].astype(F32)
            if u in DIRECT_SUM:
                h = h + buf(rs1r, u)[r : r + 32].astype(F32)
            if kind == 0:
                value, sl = gelu_and_slope(h)
                slope[chunk, r : r + 32] = sl
            else:
                value = h * slope[chunk, r : r + 32]
            ag[rows(x * Q + r, 32)] = value.astype(BF)
        free_f.append(slot_f[u])
        mine = ag.at[rows(x * Q, Q)]
        if kind == 1 and chunk in F1:
            U[u, "p"] = send(mine, pdelta.at[chunk, rows(x * Q, Q)], *usem(u, 8), dev(dy=2))
        if u in DIRECT_GATHER:
            U[u, "d", 0] = send(mine, mine, *usem(u, 6), dev(dx=2))
        U[u, "c", 0] = send(mine, mine, *usem(u, 4), dev(dx=1))
        U[u, "c", 1] = send(mine, mine, *usem(u, 5), dev(dx=3))

    def stage_d(*u):
        ag = buf(agb, u)
        U[u, "c", 0].wait_recv()
        part = ag.at[rows(lax.rem(x + 3, 4) * Q, 32)]
        U[u, "d", 0] = send(part, part, *usem(u, 6), dev(dx=1))
        U[u, "c", 1].wait_recv()
        part = ag.at[rows(lax.rem(x + 1, 4) * Q + 32, 32)]
        U[u, "d", 1] = send(part, part, *usem(u, 7), dev(dx=3))

    def stage_f1s(*u):
        part = pdelta.at[u[1], rows(x * Q, Q)]
        U[u, "p"].wait_recv()
        if u in DIRECT_GATHER:
            U[u, "pd", 0] = send(part, part, *usem(u, 14), dev(dx=2))
        U[u, "pc", 0] = send(part, part, *usem(u, 12), dev(dx=1))
        U[u, "pc", 1] = send(part, part, *usem(u, 13), dev(dx=3))

    def stage_f1r(*u):
        U[u, "pc", 0].wait_recv()
        part = pdelta.at[u[1], rows(lax.rem(x + 3, 4) * Q, 32)]
        U[u, "pd", 0] = send(part, part, *usem(u, 14), dev(dx=1))
        U[u, "pc", 1].wait_recv()
        part = pdelta.at[u[1], rows(lax.rem(x + 1, 4) * Q + 32, 32)]
        U[u, "pd", 1] = send(part, part, *usem(u, 15), dev(dx=3))

    gathered = set()

    def whole(u):
        if u not in gathered:
            gathered.add(u)
            U[u, "d", 0].wait_recv()
            if u in DIRECT_GATHER:
                U[u, "c", 0].wait_recv()
                U[u, "c", 1].wait_recv()
            else:
                U[u, "d", 1].wait_recv()

    def stage_p(*u):
        whole(u)
        U[u, "p"] = send(buf(agb, u), pdelta.at[u[1]], *usem(u, 8), dev(dy=2))

    def stage_e(*u):
        kind = u[0]
        whole(u)
        if kind == 0:
            ready(3)
        n = len(sib_sends)
        if n >= SS:
            sib_sends[n - SS].wait_send()
            waited.append(id(sib_sends[n - SS]))
        out, k = sibs.at[n % SS], keep.at[slot_k.setdefault(u, free_k.pop(0))]
        ag = buf(agb, u)
        lhs = jnp.concatenate(
            [ag[rows((1 - c) * 128, 128)], ag[rows(c * 128, 128)]], axis=0
        )
        part = jnp.dot(lhs, wb[kind], preferred_element_type=F32)
        out[...] = part[:128].astype(BF)
        U[u, "e"] = send(out, buf(sibr, u), *usem(u, 9), dev(dc=1))
        k[...] = part[128:]
        sib_sends.append(U[u, "e"])

    def stage_f(*u):
        kind, chunk = u
        U[u, "e"].wait_recv()
        k, got = keep.at[slot_k[u]], buf(sibr, u)
        relayed = kind in RELAY_Z and chunk in (1, 2)
        if relayed:
            U[kind, chunk, "zr"].wait_recv()
        for n in range(4):
            r = slice(n * B, n * B + B)
            total = k[r] + got[r].astype(F32)
            if relayed and n // 2 == chunk - 1:
                total = total + zr[kind, 2, r].astype(F32)
            if chunk == 0:
                s0[kind, r] = total
            else:
                zs[kind, chunk - 1, r] = total.astype(BF)
        free_k.append(slot_k[u])
        if kind in RELAY_Z and chunk == 3:
            for i, d in ((1, 1), (2, 3)):
                r = slice(i * 64 - 64, i * 64)
                U[kind, i, "zr"] = send(
                    zs.at[kind, 2, r], zr.at[kind, 2, r], *usem((kind, i), 11), dev(dz=d)
                )
        elif chunk != 0:
            U[kind, chunk, "z"] = send(
                zs.at[kind, chunk - 1], zr.at[kind, chunk - 1], *usem(u, 10),
                dev(dz=OFFSET[chunk]),
            )

    def stage_g(kind):
        parts = (1, 2) if kind in RELAY_Z else (1, 2, 3)
        for chunk in parts:
            U[kind, chunk, "z"].wait_recv()

        def total(blk):
            r = rows(blk * B, B)
            t = s0[kind, r]
            for i in parts:
                t = t + zr[kind, i - 1, r].astype(F32)
            return t

        for d in (1, 3, 2):
            ys[kind, d - 1] = total(lax.rem(y + d, 4)).astype(BF)
            U[kind, d, "y"] = send(
                ys.at[kind, d - 1], yr.at[kind, d - 1], fsend.at[kind, d - 1],
                frecv.at[kind, d - 1], dev(dy=d),
            )
        s0[kind, 0:B] = total(y)

    def stage_h(kind):
        t = s0[kind, 0:B]
        for d in (1, 3, 2):
            U[kind, d, "y"].wait_recv()
            t = t + yr[kind, d - 1].astype(F32)
        (lo_ref, tg_ref)[kind][...] = t.astype(BF)

    out_copies = []
    count = [0, 0]

    def lead(a, b):
        return lax.dot_general(a, b, (((0,), (0,)), ((), ())), preferred_element_type=F32)

    def stage_sg(part):
        at = slice(part * H, part * H + H)
        t = None
        for j in range(4):
            whole((0, j))
            group(1, j)
            p = lead(agb[j], xs[1, lax.rem(z + OFFSET[j], 4), :, at])
            t = p if t is None else t + p
        wb[0, :, at] = t.astype(BF)
        cp = pltpu.make_async_copy(wb.at[0, :, at], sg_ref.at[:, at], lsem.at[4 + part])
        cp.start()
        out_copies.append(cp)

    def first_grad(chunk, side, src):
        p = lead(xs[0, lax.rem(z + OFFSET[chunk], 4), :, half], src[...])
        if count[side]:
            p = p + facc[side]
        count[side] += 1
        if count[side] < 4:
            facc[side] = p
            return
        at = slice(side * H, side * H + H)
        wa[0, at, :] = p.astype(BF)
        to = rows((1 - yh if side else yh) * H, H)
        cp = pltpu.make_async_copy(wa.at[0, at], fg_ref.at[:, to], lsem.at[6 + side])
        cp.start()
        out_copies.append(cp)

    def stage_fo(chunk):
        whole((1, chunk))
        first_grad(chunk, 0, agb.at[4 + chunk])

    def stage_fp(chunk):
        u = (1, chunk)
        if chunk in F1:
            U[u, "pd", 0].wait_recv()
            if u in DIRECT_GATHER:
                U[u, "pc", 0].wait_recv()
                U[u, "pc", 1].wait_recv()
            else:
                U[u, "pd", 1].wait_recv()
        else:
            U[u, "p"].wait_recv()
        first_grad(chunk, 1, pdelta.at[chunk])

    def stage_t1():
        ready(3)
        wa[1] = wb[0].T

    def stage_t2():
        ready(2)
        wb[1] = wa[0].T

    steps = dict(
        gy=gather_y, gz=gather_z, gr=gather_relay, gl=gather_last, t1=stage_t1,
        t2=stage_t2, a=stage_a, b=stage_b, c=stage_c, d=stage_d, p=stage_p, e=stage_e,
        f=stage_f, g=stage_g, h=stage_h, sg=stage_sg, fo=stage_fo, fp=stage_fp,
        f1s=stage_f1s, f1r=stage_f1r,
    )
    for name, *args in SCHEDULE:
        steps[name](*args)
    for cp in pending:
        if id(cp) not in waited:
            cp.wait_send()
    for cp in out_copies:
        cp.wait()


def widen(lo_in, tg_in, fg_in, sg_in, lo_ref, tg_ref, fg_ref, sg_ref):
    lo_ref[...] = lo_in[...]
    tg_ref[...] = tg_in[...]
    fg_ref[...] = fg_in[...].astype(F32)
    sg_ref[...] = sg_in[...].astype(F32)


def local(tokens, first_weight, second_weight, upstream):
    vm = pl.BlockSpec(memory_space=pltpu.VMEM)
    hbm = pl.BlockSpec(memory_space=pl.ANY)
    dma = pltpu.SemaphoreType.DMA
    lo, tg, fg, sg = pl.pallas_call(
        kernel,
        out_shape=(
            jax.ShapeDtypeStruct((B, W), BF),
            jax.ShapeDtypeStruct((B, W), BF),
            jax.ShapeDtypeStruct((H, W), BF),
            jax.ShapeDtypeStruct((H, W), BF),
        ),
        in_specs=[hbm] * 4,
        out_specs=(vm, vm, hbm, hbm),
        scratch_shapes=[
            pltpu.VMEM((2, 4, C, W), BF),
            pltpu.VMEM((2, W, H), BF),
            pltpu.VMEM((2, H, W), BF),
            pltpu.VMEM((FS, C, H), F32),
            pltpu.VMEM((8, Q, H), BF),
            pltpu.VMEM((8, Q, H), BF),
            pltpu.VMEM((8, 2, Q, H), BF),
            pltpu.VMEM((8, 2, Q, H), BF),
            pltpu.VMEM((8, C, H), BF),
            pltpu.VMEM((4, Q, H), F32),
            pltpu.VMEM((4, C, H), BF),
            pltpu.VMEM((KS, 128, W), F32),
            pltpu.VMEM((SS, 128, W), BF),
            pltpu.VMEM((8, 128, W), BF),
            pltpu.VMEM((2, 3, 128, W), BF),
            pltpu.VMEM((2, 3, 128, W), BF),
            pltpu.VMEM((2, 128, W), F32),
            pltpu.VMEM((2, 3, B, W), BF),
            pltpu.VMEM((2, 3, B, W), BF),
            pltpu.VMEM((2, H, H), F32),
            dma((8,)),
            dma((2, 11)), dma((2, 11)),
            dma((8, 16)), dma((8, 16)),
            dma((2, 3)), dma((2, 3)),
        ],
        compiler_params=pltpu.CompilerParams(
            collective_id=0, has_side_effects=True, vmem_limit_bytes=60 << 20
        ),
        cost_estimate=pl.CostEstimate(
            flops=6 * 2 * 1024 * W * H, bytes_accessed=16 << 20, transcendentals=0
        ),
        name="ffn",
    )(tokens, first_weight, second_weight, upstream)
    small = pl.BlockSpec((B, W), lambda i: (0, 0))
    large = pl.BlockSpec((H // 4, W), lambda i: (i, 0))
    return pl.pallas_call(
        widen,
        grid=(4,),
        out_shape=(
            jax.ShapeDtypeStruct((B, W), BF),
            jax.ShapeDtypeStruct((B, W), BF),
            jax.ShapeDtypeStruct((H, W), F32),
            jax.ShapeDtypeStruct((H, W), F32),
        ),
        in_specs=[small, small, large, large],
        out_specs=(small, small, large, large),
        name="widen",
    )(lo, tg, fg, sg)


def solution(mesh):
    in_specs = (
        P(("col", "depth"), "row"),
        P("row", "col"),
        P("col", "row"),
        P(("col", "depth"), "row"),
    )
    out_specs = (
        P(("col", "depth"), "row"),
        P(("col", "depth"), "row"),
        P(("row", "depth"), "col"),
        P(("col", "depth"), "row"),
    )
    return jax.shard_map(local, mesh=mesh, in_specs=in_specs, out_specs=out_specs, check_vma=False)
```

```python
import math

import jax
import jax.numpy as jnp
from jax import lax
from jax.experimental import pallas as pl
from jax.experimental.pallas import tpu as pltpu
from jax.sharding import PartitionSpec as P

MESH = pl.DeviceIdType.MESH
BF = jnp.bfloat16
F32 = jnp.float32
SCALE = math.sqrt(2.0 / math.pi)

W = 1792
H = 896
C = 256
Q = 64
B = 32
OFFSET = (0, 1, 3, 2)
DIRECT_SUM = ((0, 0),)
DIRECT_GATHER = ((1, 0), (1, 2))
FS, KS, SS = 3, 4, 4
RELAY_Z = (0, 1)
F1 = (0, 1, 2)

SCHEDULE = (
    ("gy", 0), ("gz", 0), ("gy", 1), ("gz2", 0), ("gz1", 0), ("gz", 1), ("a", 0, 0), ("t1",),
    ("gr", 0, 2), ("gr", 0, 1), ("a", 0, 2), ("gz1", 1), ("c", 0, 0), ("b", 0, 2), ("gl", 0),
    ("a", 0, 1), ("a", 0, 3), ("gz2", 1), ("c", 0, 2), ("b", 0, 3), ("b", 0, 1), ("gr", 1, 1),
    ("gr", 1, 2), ("a", 1, 1), ("c", 0, 3), ("c", 0, 1), ("t2",), ("gl", 1), ("d", 0, 3),
    ("a", 1, 3), ("d", 0, 2), ("d", 0, 1), ("b", 1, 1), ("e", 0, 3), ("b", 1, 3), ("a", 1, 2),
    ("f", 0, 3), ("e", 0, 1), ("c", 1, 1), ("e", 0, 2), ("c", 1, 3), ("f", 0, 2), ("b", 1, 2),
    ("f", 0, 1), ("d", 1, 3), ("d", 1, 1), ("a", 1, 0), ("c", 1, 2), ("e", 1, 3), ("fo", 3),
    ("f", 1, 3), ("p", 1, 3), ("b", 1, 0), ("d", 0, 0), ("f1s", 1, 1), ("e", 1, 1),
    ("e", 1, 2), ("c", 1, 0), ("f", 1, 1), ("f", 1, 2), ("e", 0, 0), ("f", 0, 0), ("g", 0),
    ("f1s", 1, 2), ("sg", 1), ("e", 1, 0), ("f1s", 1, 0), ("f", 1, 0), ("fo", 2), ("h", 0),
    ("g", 1), ("f1r", 1, 1), ("fo", 0), ("sg", 0), ("fp", 2), ("fo", 1), ("fp", 0), ("fp", 3),
    ("fp", 1), ("h", 1),
)


def gelu_and_slope(h):
    inner = SCALE * (h + 0.044715 * h * h * h)
    t = jnp.tanh(inner)
    value = 0.5 * h * (1.0 + t)
    slope = 0.5 * (1.0 + t) + 0.5 * h * (1.0 - t * t) * SCALE * (
        1.0 + 3.0 * 0.044715 * h * h
    )
    return value, slope


def kernel(
    tok_ref, w1_ref, w2_ref, up_ref,
    lo_ref, tg_ref, fg_ref, sg_ref,
    xs, wa, wb, hp, rs1s, rs1r, rs2s, rs2r, agb, slope, pdelta,
    keep, sibs, sibr, zs, zr, s0, ys, yr, facc,
    lsem, gsend, grecv, usend, urecv, fsend, frecv,
):
    x = lax.axis_index("row")
    col = lax.axis_index("col")
    yh = lax.axis_index("depth")
    z, yl, c = col // 4, (col // 2) % 2, col % 2
    y = yh * 2 + yl

    def dev(dx=0, dy=0, dz=0, dc=0):
        xx, yy = lax.rem(x + dx, 4), lax.rem(y + dy, 4)
        zz, cc = lax.rem(z + dz, 4), lax.rem(c + dc, 2)
        return (xx, zz * 4 + lax.rem(yy, 2) * 2 + cc, yy // 2)

    pending, waited = [], []

    def send(src, dst, ss, rs, to):
        cp = pltpu.make_async_remote_copy(
            src_ref=src, dst_ref=dst, send_sem=ss, recv_sem=rs,
            device_id=to, device_id_type=MESH,
        )
        cp.start()
        pending.append(cp)
        return cp

    def rows(start, size):
        return pl.ds(pl.multiple_of(start, size), size)

    half = rows(yh * H, H)
    in_copies = [
        pltpu.make_async_copy(tok_ref, xs.at[0, z, rows(c * 128 + y * B, B)], lsem.at[0]),
        pltpu.make_async_copy(up_ref, xs.at[1, z, rows(c * 128 + y * B, B)], lsem.at[1]),
        pltpu.make_async_copy(w1_ref.at[:, half], wa.at[0], lsem.at[2]),
        pltpu.make_async_copy(w2_ref.at[half, :], wb.at[0], lsem.at[3]),
    ]
    for cp in in_copies:
        cp.start()
    loaded = set()

    def ready(i):
        if i not in loaded:
            loaded.add(i)
            in_copies[i].wait()

    barrier = pltpu.get_barrier_semaphore()
    peers = [dev(dc=1), dev(dx=1), dev(dx=2), dev(dx=3), dev(dy=1), dev(dy=2), dev(dy=3),
             dev(dz=1), dev(dz=2), dev(dz=3)]
    for p in peers:
        pl.semaphore_signal(barrier, inc=1, device_id=p, device_id_type=MESH)
    pl.semaphore_wait(barrier, len(peers))

    G = {}

    def gsem(k, i):
        return gsend.at[k, i], grecv.at[k, i]

    def gather_y(k):
        ready(k)
        blk = xs.at[k, z, rows(c * 128 + y * B, B)]
        for d in (2, 1, 3):
            G[k, "y", d] = send(blk, blk, *gsem(k, d - 1), dev(dy=d))

    def forward(k, d):
        blk = xs.at[k, z, rows(c * 128 + lax.rem(y + d, 4) * B, B)]
        G[k, "s0", d] = send(blk, blk, *gsem(k, 3 + d), dev(dc=1))
        G[k, "z", 1, d] = send(blk, blk, *gsem(k, 7 + d), dev(dz=1))
        G[k, "z", 3, d] = send(blk, blk, *gsem(k, 11 + d), dev(dz=3))

    def gather_z0(k):
        forward(k, 0)

    def gather_z1(k):
        for d in (1, 3):
            G[k, "y", d].wait_recv()
            forward(k, 4 - d)

    def gather_z2(k):
        G[k, "y", 2].wait_recv()
        forward(k, 2)

    def gather_relay(k, chunk):
        zz = lax.rem(z + OFFSET[chunk], 4)
        for d in range(4):
            G[k, "z", 3 if chunk == 1 else 1, d].wait_recv()
        if chunk == 1:
            part = xs.at[k, zz, rows(c * 128 + 64, 64)]
            G[k, "r", 1] = send(part, part, *gsem(k, 15), dev(dz=3))
        else:
            part = xs.at[k, zz, rows(c * 128, 64)]
            G[k, "r", 2] = send(part, part, *gsem(k, 16), dev(dz=1))
        grp = xs.at[k, zz, rows(c * 128, 128)]
        G[k, "s", chunk] = send(grp, grp, *gsem(k, 16 + chunk), dev(dc=1))

    def gather_last(k):
        G[k, "r", 1].wait_recv()
        G[k, "r", 2].wait_recv()
        grp = xs.at[k, lax.rem(z + 2, 4), rows(c * 128, 128)]
        G[k, "s", 3] = send(grp, grp, *gsem(k, 19), dev(dc=1))

    grouped = set()

    def group(k, chunk):
        if (k, chunk) not in grouped:
            grouped.add((k, chunk))
            if chunk == 0:
                for d in range(4):
                    G[k, "s0", d].wait_recv()
            else:
                G[k, "s", chunk].wait_recv()

    U = {}
    free_f, free_k, sib_sends = list(range(FS)), list(range(KS)), []
    slot_f, slot_k = {}, {}

    def usem(u, i):
        n = u[0] * 4 + u[1]
        return usend.at[n, i], urecv.at[n, i]

    def buf(ref, u):
        return ref.at[u[0] * 4 + u[1]]

    def stage_a(*u):
        kind, chunk = u
        group(kind, chunk)
        if kind == 0:
            ready(2)
        zz = lax.rem(z + OFFSET[chunk], 4)
        f = hp.at[slot_f.setdefault(u, free_f.pop(0))]
        f[...] = jnp.dot(xs[kind, zz], wa[kind], preferred_element_type=F32)
        away, into = buf(rs1s, u), buf(rs1r, u)
        away[...] = f[rows(lax.rem(x + 2, 4) * Q, Q)].astype(BF)
        if u in DIRECT_SUM:
            U[u, "a", 0] = send(away, into, *usem(u, 0), dev(dx=2))
            out, into = buf(rs2s, u), buf(rs2r, u)
            out[0] = f[rows(lax.rem(x + 1, 4) * Q, Q)].astype(BF)
            U[u, "b", 0] = send(out.at[0], into.at[0], *usem(u, 2), dev(dx=1))
            out[1] = f[rows(lax.rem(x + 3, 4) * Q, Q)].astype(BF)
            U[u, "b", 1] = send(out.at[1], into.at[1], *usem(u, 3), dev(dx=3))
            return
        U[u, "a", 0] = send(away.at[0:32], into.at[0:32], *usem(u, 0), dev(dx=1))
        U[u, "a", 1] = send(away.at[32:64], into.at[32:64], *usem(u, 1), dev(dx=3))

    def stage_b(*u):
        f = hp.at[slot_f[u]]
        right, left = lax.rem(x + 1, 4) * Q, lax.rem(x + 3, 4) * Q
        out, got, into = buf(rs2s, u), buf(rs1r, u), buf(rs2r, u)
        U[u, "a", 0].wait_recv()
        out[0, 0:32] = (f[rows(right, 32)] + got[0:32].astype(F32)).astype(BF)
        out[0, 32:64] = f[rows(right + 32, 32)].astype(BF)
        U[u, "b", 0] = send(out.at[0], into.at[0], *usem(u, 2), dev(dx=1))
        U[u, "a", 1].wait_recv()
        out[1, 0:32] = f[rows(left, 32)].astype(BF)
        out[1, 32:64] = (f[rows(left + 32, 32)] + got[32:64].astype(F32)).astype(BF)
        U[u, "b", 1] = send(out.at[1], into.at[1], *usem(u, 3), dev(dx=3))

    def stage_c(*u):
        kind, chunk = u
        f, got, ag = hp.at[slot_f[u]], buf(rs2r, u), buf(agb, u)
        U[u, "b", 0].wait_recv()
        U[u, "b", 1].wait_recv()
        if u in DIRECT_SUM:
            U[u, "a", 0].wait_recv()
        for r in range(0, Q, 32):
            h = f[rows(x * Q + r, 32)]
            h = h + got[0, r : r + 32].astype(F32) + got[1, r : r + 32].astype(F32)
            if u in DIRECT_SUM:
                h = h + buf(rs1r, u)[r : r + 32].astype(F32)
            if kind == 0:
                value, sl = gelu_and_slope(h)
                slope[chunk, r : r + 32] = sl
            else:
                value = h * slope[chunk, r : r + 32]
            ag[rows(x * Q + r, 32)] = value.astype(BF)
        free_f.append(slot_f[u])
        mine = ag.at[rows(x * Q, Q)]
        if kind == 1 and chunk in F1:
            U[u, "p"] = send(mine, pdelta.at[chunk, rows(x * Q, Q)], *usem(u, 8), dev(dy=2))
        if u in DIRECT_GATHER:
            U[u, "d", 0] = send(mine, mine, *usem(u, 6), dev(dx=2))
        U[u, "c", 0] = send(mine, mine, *usem(u, 4), dev(dx=1))
        U[u, "c", 1] = send(mine, mine, *usem(u, 5), dev(dx=3))

    def stage_d(*u):
        ag = buf(agb, u)
        U[u, "c", 0].wait_recv()
        part = ag.at[rows(lax.rem(x + 3, 4) * Q, 32)]
        U[u, "d", 0] = send(part, part, *usem(u, 6), dev(dx=1))
        U[u, "c", 1].wait_recv()
        part = ag.at[rows(lax.rem(x + 1, 4) * Q + 32, 32)]
        U[u, "d", 1] = send(part, part, *usem(u, 7), dev(dx=3))

    def stage_f1s(*u):
        part = pdelta.at[u[1], rows(x * Q, Q)]
        U[u, "p"].wait_recv()
        if u in DIRECT_GATHER:
            U[u, "pd", 0] = send(part, part, *usem(u, 14), dev(dx=2))
        U[u, "pc", 0] = send(part, part, *usem(u, 12), dev(dx=1))
        U[u, "pc", 1] = send(part, part, *usem(u, 13), dev(dx=3))

    def stage_f1r(*u):
        U[u, "pc", 0].wait_recv()
        part = pdelta.at[u[1], rows(lax.rem(x + 3, 4) * Q, 32)]
        U[u, "pd", 0] = send(part, part, *usem(u, 14), dev(dx=1))
        U[u, "pc", 1].wait_recv()
        part = pdelta.at[u[1], rows(lax.rem(x + 1, 4) * Q + 32, 32)]
        U[u, "pd", 1] = send(part, part, *usem(u, 15), dev(dx=3))

    gathered = set()

    def whole(u):
        if u not in gathered:
            gathered.add(u)
            U[u, "d", 0].wait_recv()
            if u in DIRECT_GATHER:
                U[u, "c", 0].wait_recv()
                U[u, "c", 1].wait_recv()
            else:
                U[u, "d", 1].wait_recv()

    def stage_p(*u):
        whole(u)
        U[u, "p"] = send(buf(agb, u), pdelta.at[u[1]], *usem(u, 8), dev(dy=2))

    def stage_e(*u):
        kind = u[0]
        whole(u)
        if kind == 0:
            ready(3)
        n = len(sib_sends)
        if n >= SS:
            sib_sends[n - SS].wait_send()
            waited.append(id(sib_sends[n - SS]))
        out, k = sibs.at[n % SS], keep.at[slot_k.setdefault(u, free_k.pop(0))]
        ag = buf(agb, u)
        lhs = jnp.concatenate(
            [ag[rows((1 - c) * 128, 128)], ag[rows(c * 128, 128)]], axis=0
        )
        part = jnp.dot(lhs, wb[kind], preferred_element_type=F32)
        out[...] = part[:128].astype(BF)
        U[u, "e"] = send(out, buf(sibr, u), *usem(u, 9), dev(dc=1))
        k[...] = part[128:]
        sib_sends.append(U[u, "e"])

    def stage_f(*u):
        kind, chunk = u
        U[u, "e"].wait_recv()
        k, got = keep.at[slot_k[u]], buf(sibr, u)
        relayed = kind in RELAY_Z and chunk in (1, 2)
        if relayed:
            U[kind, chunk, "zr"].wait_recv()
        for n in range(4):
            r = slice(n * B, n * B + B)
            total = k[r] + got[r].astype(F32)
            if relayed and n // 2 == chunk - 1:
                total = total + zr[kind, 2, r].astype(F32)
            if chunk == 0:
                s0[kind, r] = total
            else:
                zs[kind, chunk - 1, r] = total.astype(BF)
        free_k.append(slot_k[u])
        if kind in RELAY_Z and chunk == 3:
            for i, d in ((1, 1), (2, 3)):
                r = slice(i * 64 - 64, i * 64)
                U[kind, i, "zr"] = send(
                    zs.at[kind, 2, r], zr.at[kind, 2, r], *usem((kind, i), 11), dev(dz=d)
                )
        elif chunk != 0:
            U[kind, chunk, "z"] = send(
                zs.at[kind, chunk - 1], zr.at[kind, chunk - 1], *usem(u, 10),
                dev(dz=OFFSET[chunk]),
            )

    def stage_g(kind):
        parts = (1, 2) if kind in RELAY_Z else (1, 2, 3)
        for chunk in parts:
            U[kind, chunk, "z"].wait_recv()

        def total(blk):
            r = rows(blk * B, B)
            t = s0[kind, r]
            for i in parts:
                t = t + zr[kind, i - 1, r].astype(F32)
            return t

        for d in (2, 1, 3):
            ys[kind, d - 1] = total(lax.rem(y + d, 4)).astype(BF)
            U[kind, d, "y"] = send(
                ys.at[kind, d - 1], yr.at[kind, d - 1], fsend.at[kind, d - 1],
                frecv.at[kind, d - 1], dev(dy=d),
            )
        s0[kind, 0:B] = total(y)

    def stage_h(kind):
        t = s0[kind, 0:B]
        for d in (1, 3, 2):
            U[kind, d, "y"].wait_recv()
            t = t + yr[kind, d - 1].astype(F32)
        (lo_ref, tg_ref)[kind][...] = t.astype(BF)

    out_copies = []
    count = [0, 0]

    def lead(a, b):
        return lax.dot_general(a, b, (((0,), (0,)), ((), ())), preferred_element_type=F32)

    def stage_sg(part):
        at = slice(part * H, part * H + H)
        t = None
        for j in range(4):
            whole((0, j))
            group(1, j)
            p = lead(agb[j], xs[1, lax.rem(z + OFFSET[j], 4), :, at])
            t = p if t is None else t + p
        wb[0, :, at] = t.astype(BF)
        cp = pltpu.make_async_copy(wb.at[0, :, at], sg_ref.at[:, at], lsem.at[4 + part])
        cp.start()
        out_copies.append(cp)

    def first_grad(chunk, side, src):
        p = lead(xs[0, lax.rem(z + OFFSET[chunk], 4), :, half], src[...])
        if count[side]:
            p = p + facc[side]
        count[side] += 1
        if count[side] < 4:
            facc[side] = p
            return
        at = slice(side * H, side * H + H)
        wa[0, at, :] = p.astype(BF)
        to = rows((1 - yh if side else yh) * H, H)
        cp = pltpu.make_async_copy(wa.at[0, at], fg_ref.at[:, to], lsem.at[6 + side])
        cp.start()
        out_copies.append(cp)

    def stage_fo(chunk):
        whole((1, chunk))
        first_grad(chunk, 0, agb.at[4 + chunk])

    def stage_fp(chunk):
        u = (1, chunk)
        if chunk in F1:
            U[u, "pd", 0].wait_recv()
            if u in DIRECT_GATHER:
                U[u, "pc", 0].wait_recv()
                U[u, "pc", 1].wait_recv()
            else:
                U[u, "pd", 1].wait_recv()
        else:
            U[u, "p"].wait_recv()
        first_grad(chunk, 1, pdelta.at[chunk])

    def stage_t1():
        ready(3)
        wa[1] = wb[0].T

    def stage_t2():
        ready(2)
        wb[1] = wa[0].T

    steps = dict(
        gy=gather_y, gz=gather_z0, gz1=gather_z1, gz2=gather_z2,
        gr=gather_relay, gl=gather_last, t1=stage_t1,
        t2=stage_t2, a=stage_a, b=stage_b, c=stage_c, d=stage_d, p=stage_p, e=stage_e,
        f=stage_f, g=stage_g, h=stage_h, sg=stage_sg, fo=stage_fo, fp=stage_fp,
        f1s=stage_f1s, f1r=stage_f1r,
    )
    for name, *args in SCHEDULE:
        steps[name](*args)
    for cp in pending:
        if id(cp) not in waited:
            cp.wait_send()
    for cp in out_copies:
        cp.wait()


def widen(
    lo_in, tg_in, fg_in, sg_in, lo_ref, tg_ref, fg_ref, sg_ref,
    narrow, wide, small_sem, in_sem, out_sem,
):
    small = [
        pltpu.make_async_copy(lo_in, lo_ref, small_sem.at[0]),
        pltpu.make_async_copy(tg_in, tg_ref, small_sem.at[1]),
    ]
    ins, outs = [], []
    size = H // 4
    for i in range(4):
        for a, src in enumerate((fg_in, sg_in)):
            r = slice(i * size, i * size + size)
            cp = pltpu.make_async_copy(src.at[r], narrow.at[a, r], in_sem.at[a, i])
            cp.start()
            ins.append((a, i, r, cp))
    for cp in small:
        cp.start()
    for a, i, r, cp in ins:
        cp.wait()
        wide[a, r] = narrow[a, r].astype(F32)
        dst = (fg_ref, sg_ref)[a]
        out = pltpu.make_async_copy(wide.at[a, r], dst.at[r], out_sem.at[a, i])
        out.start()
        outs.append(out)
    for cp in outs + small:
        cp.wait()


def local(tokens, first_weight, second_weight, upstream):
    vm = pl.BlockSpec(memory_space=pltpu.VMEM)
    hbm = pl.BlockSpec(memory_space=pl.ANY)
    dma = pltpu.SemaphoreType.DMA
    lo, tg, fg, sg = pl.pallas_call(
        kernel,
        out_shape=(
            jax.ShapeDtypeStruct((B, W), BF),
            jax.ShapeDtypeStruct((B, W), BF),
            jax.ShapeDtypeStruct((H, W), BF),
            jax.ShapeDtypeStruct((H, W), BF),
        ),
        in_specs=[hbm] * 4,
        out_specs=(vm, vm, hbm, hbm),
        scratch_shapes=[
            pltpu.VMEM((2, 4, C, W), BF),
            pltpu.VMEM((2, W, H), BF),
            pltpu.VMEM((2, H, W), BF),
            pltpu.VMEM((FS, C, H), F32),
            pltpu.VMEM((8, Q, H), BF),
            pltpu.VMEM((8, Q, H), BF),
            pltpu.VMEM((8, 2, Q, H), BF),
            pltpu.VMEM((8, 2, Q, H), BF),
            pltpu.VMEM((8, C, H), BF),
            pltpu.VMEM((4, Q, H), F32),
            pltpu.VMEM((4, C, H), BF),
            pltpu.VMEM((KS, 128, W), F32),
            pltpu.VMEM((SS, 128, W), BF),
            pltpu.VMEM((8, 128, W), BF),
            pltpu.VMEM((2, 3, 128, W), BF),
            pltpu.VMEM((2, 3, 128, W), BF),
            pltpu.VMEM((2, 128, W), F32),
            pltpu.VMEM((2, 3, B, W), BF),
            pltpu.VMEM((2, 3, B, W), BF),
            pltpu.VMEM((2, H, H), F32),
            dma((8,)),
            dma((2, 20)), dma((2, 20)),
            dma((8, 16)), dma((8, 16)),
            dma((2, 3)), dma((2, 3)),
        ],
        compiler_params=pltpu.CompilerParams(
            collective_id=0, has_side_effects=True, vmem_limit_bytes=60 << 20
        ),
        cost_estimate=pl.CostEstimate(
            flops=6 * 2 * 1024 * W * H, bytes_accessed=16 << 20, transcendentals=0
        ),
        name="ffn",
    )(tokens, first_weight, second_weight, upstream)
    return pl.pallas_call(
        widen,
        out_shape=(
            jax.ShapeDtypeStruct((B, W), BF),
            jax.ShapeDtypeStruct((B, W), BF),
            jax.ShapeDtypeStruct((H, W), F32),
            jax.ShapeDtypeStruct((H, W), F32),
        ),
        in_specs=[hbm] * 4,
        out_specs=(hbm,) * 4,
        scratch_shapes=[
            pltpu.VMEM((2, H, W), BF), pltpu.VMEM((2, H, W), F32),
            dma((2,)), dma((2, 4)), dma((2, 4)),
        ],
        compiler_params=pltpu.CompilerParams(vmem_limit_bytes=40 << 20),
        name="widen",
    )(lo, tg, fg, sg)


def solution(mesh):
    in_specs = (
        P(("col", "depth"), "row"),
        P("row", "col"),
        P("col", "row"),
        P(("col", "depth"), "row"),
    )
    out_specs = (
        P(("col", "depth"), "row"),
        P(("col", "depth"), "row"),
        P(("row", "depth"), "col"),
        P(("col", "depth"), "row"),
    )
    return jax.shard_map(local, mesh=mesh, in_specs=in_specs, out_specs=out_specs, check_vma=False)
```

```python
import math

import jax
import jax.numpy as jnp
from jax import lax
from jax.experimental import pallas as pl
from jax.experimental.pallas import tpu as pltpu
from jax.sharding import PartitionSpec as P

MESH = pl.DeviceIdType.MESH
BF = jnp.bfloat16
F32 = jnp.float32
SCALE = math.sqrt(2.0 / math.pi)

W = 1792
H = 896
C = 256
Q = 64
B = 32
OFFSET = (0, 1, 3, 2)
DIRECT_SUM = ((0, 0), (0, 4), (1, 0), (1, 4))
DIRECT_GATHER = ((1, 1), (1, 2), (1, 4))
FS, KS, SS = 4, 4, 4
RELAY_Z = (1,)
F1 = (1, 2, 4)

SCHEDULE = (
    ("gy", 0), ("t1",), ("gz", 0), ("gz1", 0), ("gy", 1), ("a", 0, 0), ("gz2", 0), ("gz", 1),
    ("a", 0, 4), ("gz1", 1), ("a", 1, 0), ("gr", 0, 2), ("c", 0, 0), ("gr", 0, 1),
    ("c", 0, 4), ("gz2", 1), ("a", 0, 2), ("c", 1, 0), ("a", 0, 1), ("b", 0, 2), ("d", 0, 0),
    ("b", 0, 1), ("gl", 0), ("c", 0, 2), ("a", 0, 3), ("gr", 1, 1), ("c", 0, 1), ("gr", 1, 2),
    ("d", 0, 2), ("a", 1, 1), ("b", 0, 3), ("d", 0, 1), ("a", 1, 2), ("gl", 1), ("e", 0, 2),
    ("a", 1, 3), ("c", 0, 3), ("e", 0, 1), ("f", 0, 2), ("b", 1, 3), ("f", 0, 1), ("t2",),
    ("d", 0, 3), ("b", 1, 2), ("e", 0, 0), ("c", 1, 3), ("e", 0, 3), ("b", 1, 1), ("f", 0, 3),
    ("d", 1, 3), ("c", 1, 2), ("c", 1, 1), ("d", 1, 0), ("f", 0, 0), ("d", 0, 4), ("a", 1, 4),
    ("e", 1, 3), ("p", 1, 3), ("f", 1, 3), ("e", 1, 2), ("e", 1, 1), ("f1s", 1, 1),
    ("e", 0, 4), ("f", 1, 2), ("p", 1, 0), ("f", 1, 1), ("sg", 0), ("f", 0, 4), ("c", 1, 4),
    ("g", 0, 0), ("e", 1, 0), ("fo", 2), ("g", 0, 4), ("f1s", 1, 2), ("fo", 1), ("f", 1, 0),
    ("fp", 1), ("e", 1, 4), ("f1s", 1, 4), ("fo", 0), ("fp", 0), ("f", 1, 4), ("fp", 3),
    ("g", 1, 4), ("g", 1, 0), ("sg", 1), ("fp", 2), ("fo", 3), ("h", 0), ("fo", 4), ("fp", 4),
    ("h", 1),
)


def gelu_and_slope(h):
    inner = SCALE * (h + 0.044715 * h * h * h)
    t = jnp.tanh(inner)
    value = 0.5 * h * (1.0 + t)
    slope = 0.5 * (1.0 + t) + 0.5 * h * (1.0 - t * t) * SCALE * (
        1.0 + 3.0 * 0.044715 * h * h
    )
    return value, slope


def kernel(
    tok_ref, w1_ref, w2_ref, up_ref,
    lo_ref, tg_ref, fg_ref, sg_ref,
    xs, wa, wb, hp, rs1s, rs1r, rs2s, rs2r, agb, slope, pdelta,
    keep, sibs, sibr, zr, s0, ys, yr, facc,
    lsem, gsend, grecv, usend, urecv, fsend, frecv,
):
    x = lax.axis_index("row")
    col = lax.axis_index("col")
    yh = lax.axis_index("depth")
    z, yl, c = col // 4, (col // 2) % 2, col % 2
    y = yh * 2 + yl

    def dev(dx=0, dy=0, dz=0, dc=0):
        xx, yy = lax.rem(x + dx, 4), lax.rem(y + dy, 4)
        zz, cc = lax.rem(z + dz, 4), lax.rem(c + dc, 2)
        return (xx, zz * 4 + lax.rem(yy, 2) * 2 + cc, yy // 2)

    pending, waited = [], []

    def send(src, dst, ss, rs, to):
        cp = pltpu.make_async_remote_copy(
            src_ref=src, dst_ref=dst, send_sem=ss, recv_sem=rs,
            device_id=to, device_id_type=MESH,
        )
        cp.start()
        pending.append(cp)
        return cp

    def rows(start, size):
        return pl.ds(pl.multiple_of(start, size), size)

    half = rows(yh * H, H)
    in_copies = [
        pltpu.make_async_copy(tok_ref, xs.at[0, z, rows(c * 128 + y * B, B)], lsem.at[0]),
        pltpu.make_async_copy(up_ref, xs.at[1, z, rows(c * 128 + y * B, B)], lsem.at[1]),
        pltpu.make_async_copy(w1_ref.at[:, half], wa.at[0], lsem.at[2]),
        pltpu.make_async_copy(w2_ref.at[half, :], wb.at[0], lsem.at[3]),
    ]
    for cp in in_copies:
        cp.start()
    loaded = set()

    def ready(i):
        if i not in loaded:
            loaded.add(i)
            in_copies[i].wait()

    barrier = pltpu.get_barrier_semaphore()
    peers = [dev(dc=1), dev(dx=1), dev(dx=2), dev(dx=3), dev(dy=1), dev(dy=2), dev(dy=3),
             dev(dz=1), dev(dz=2), dev(dz=3)]
    for p in peers:
        pl.semaphore_signal(barrier, inc=1, device_id=p, device_id_type=MESH)
    pl.semaphore_wait(barrier, len(peers))

    G = {}

    def gsem(k, i):
        return gsend.at[k, i], grecv.at[k, i]

    SHIFT = (0, 1 + 2 * yl, 2, 3 - 2 * yl)

    def gather_y(k):
        ready(k)
        blk = xs.at[k, z, rows(c * 128 + y * B, B)]
        for d in (1, 3, 2):
            G[k, "y", d] = send(blk, blk, *gsem(k, d - 1), dev(dy=SHIFT[d]))

    def forward(k, d):
        blk = xs.at[k, z, rows(c * 128 + lax.rem(y + SHIFT[d], 4) * B, B)]
        G[k, "s0", d] = send(blk, blk, *gsem(k, 3 + d), dev(dc=1))
        G[k, "z", 1, d] = send(blk, blk, *gsem(k, 7 + d), dev(dz=1))
        G[k, "z", 3, d] = send(blk, blk, *gsem(k, 11 + d), dev(dz=3))

    def gather_z0(k):
        forward(k, 0)

    def gather_z1(k):
        G[k, "y", 1].wait_recv()
        forward(k, 1)

    def gather_z2(k):
        for d in (3, 2):
            G[k, "y", d].wait_recv()
            forward(k, d)

    def gather_relay(k, chunk):
        zz = lax.rem(z + OFFSET[chunk], 4)
        for d in range(4):
            G[k, "z", 3 if chunk == 1 else 1, d].wait_recv()
        if chunk == 1:
            part = xs.at[k, zz, rows(c * 128 + 64, 64)]
            G[k, "r", 1] = send(part, part, *gsem(k, 15), dev(dz=3))
        else:
            part = xs.at[k, zz, rows(c * 128, 64)]
            G[k, "r", 2] = send(part, part, *gsem(k, 16), dev(dz=1))
        grp = xs.at[k, zz, rows(c * 128, 128)]
        G[k, "s", chunk] = send(grp, grp, *gsem(k, 16 + chunk), dev(dc=1))

    def gather_last(k):
        G[k, "r", 1].wait_recv()
        G[k, "r", 2].wait_recv()
        grp = xs.at[k, lax.rem(z + 2, 4), rows(c * 128, 128)]
        G[k, "s", 3] = send(grp, grp, *gsem(k, 19), dev(dc=1))

    grouped = set()

    def group(k, chunk):
        if (k, chunk) not in grouped:
            grouped.add((k, chunk))
            if chunk in (0, 4):
                for d in ((0, 1) if chunk == 0 else (3, 2)):
                    G[k, "s0", d].wait_recv()
            else:
                G[k, "s", chunk].wait_recv()

    U = {}
    free_f, free_k, sib_sends = list(range(FS)), list(range(KS)), []
    slot_f, slot_k = {}, {}

    def usem(u, i):
        n = u[0] * 5 + u[1]
        return usend.at[n, i], urecv.at[n, i]

    def size(u):
        return C // 2 if u[1] in (0, 4) else C

    def buf(ref, u, part=1, lead=()):
        m = size(u) // part
        start = m if u[1] == 4 else 0
        return ref.at[(u[0] * 4 + u[1] % 4,) + lead + (slice(start, start + m),)]

    def pd(u):
        return buf(pdelta, (0, u[1]))

    def tokens(k, chunk, other=False, lanes=slice(None)):
        if chunk in (0, 4):
            h = yh if (chunk == 0) != other else 1 - yh
            return jnp.concatenate(
                [xs[k, z, rows(cc * 128 + h * 64, 64), lanes] for cc in (0, 1)], axis=0
            )
        return xs[k, lax.rem(z + OFFSET[chunk], 4), :, lanes]

    def stage_a(*u):
        kind, chunk = u
        group(kind, chunk)
        if kind == 0:
            ready(2)
        q = size(u) // 4
        e = q // 2
        f = hp.at[slot_f.setdefault(u, free_f.pop(0)), 0 : size(u)]
        f[...] = jnp.dot(tokens(kind, chunk), wa[kind], preferred_element_type=F32)
        away, into = buf(rs1s, u, 4), buf(rs1r, u, 4)
        away[...] = f[rows(lax.rem(x + 2, 4) * q, q)].astype(BF)
        if u in DIRECT_SUM:
            U[u, "a", 0] = send(away, into, *usem(u, 0), dev(dx=2))
            for i, d in enumerate((1, 3)):
                out, into = buf(rs2s, u, 4, (i,)), buf(rs2r, u, 4, (i,))
                out[...] = f[rows(lax.rem(x + d, 4) * q, q)].astype(BF)
                U[u, "b", i] = send(out, into, *usem(u, 2 + i), dev(dx=d))
            return
        U[u, "a", 0] = send(away.at[0:e], into.at[0:e], *usem(u, 0), dev(dx=1))
        U[u, "a", 1] = send(away.at[e:q], into.at[e:q], *usem(u, 1), dev(dx=3))

    def stage_b(*u):
        q = size(u) // 4
        e = q // 2
        f, got = hp.at[slot_f[u], 0 : size(u)], buf(rs1r, u, 4)
        for i, d in enumerate((1, 3)):
            out, into = buf(rs2s, u, 4, (i,)), buf(rs2r, u, 4, (i,))
            start = lax.rem(x + d, 4) * q
            r, o = (slice(0, e), slice(e, q))[:: 1 - 2 * i]
            U[u, "a", i].wait_recv()
            out[r] = (f[rows(start + i * e, e)] + got[r].astype(F32)).astype(BF)
            out[o] = f[rows(start + e - i * e, e)].astype(BF)
            U[u, "b", i] = send(out, into, *usem(u, 2 + i), dev(dx=d))

    def stage_c(*u):
        kind, chunk = u
        q = size(u) // 4
        f, ag = hp.at[slot_f[u], 0 : size(u)], buf(agb, u)
        right, left = buf(rs2r, u, 4, (0,)), buf(rs2r, u, 4, (1,))
        sl_ref = buf(slope, (0, chunk), 4)
        U[u, "b", 0].wait_recv()
        U[u, "b", 1].wait_recv()
        if u in DIRECT_SUM:
            U[u, "a", 0].wait_recv()
        for n in range(0, q, 32):
            r = slice(n, n + 32)
            h = f[rows(x * q + n, 32)] + right[r].astype(F32) + left[r].astype(F32)
            if u in DIRECT_SUM:
                h = h + buf(rs1r, u, 4)[r].astype(F32)
            if kind == 0:
                value, sl = gelu_and_slope(h)
                sl_ref[r] = sl
            else:
                value = h * sl_ref[r]
            ag[rows(x * q + n, 32)] = value.astype(BF)
        free_f.append(slot_f[u])
        mine = ag.at[rows(x * q, q)]
        if kind == 1 and chunk in F1:
            U[u, "p"] = send(mine, pd(u).at[rows(x * q, q)], *usem(u, 8), dev(dy=2))
        if u in DIRECT_GATHER:
            U[u, "d", 0] = send(mine, mine, *usem(u, 6), dev(dx=2))
        U[u, "c", 0] = send(mine, mine, *usem(u, 4), dev(dx=1))
        U[u, "c", 1] = send(mine, mine, *usem(u, 5), dev(dx=3))

    def pass_on(u, ref, first, then, sem):
        q = size(u) // 4
        e = q // 2
        U[u, first, 0].wait_recv()
        part = ref.at[rows(lax.rem(x + 3, 4) * q, e)]
        U[u, then, 0] = send(part, part, *usem(u, sem), dev(dx=1))
        U[u, first, 1].wait_recv()
        part = ref.at[rows(lax.rem(x + 1, 4) * q + e, e)]
        U[u, then, 1] = send(part, part, *usem(u, sem + 1), dev(dx=3))

    def stage_d(*u):
        pass_on(u, buf(agb, u), "c", "d", 6)

    def stage_f1s(*u):
        q = size(u) // 4
        part = pd(u).at[rows(x * q, q)]
        U[u, "p"].wait_recv()
        if u in DIRECT_GATHER:
            U[u, "pd", 0] = send(part, part, *usem(u, 14), dev(dx=2))
        U[u, "pc", 0] = send(part, part, *usem(u, 12), dev(dx=1))
        U[u, "pc", 1] = send(part, part, *usem(u, 13), dev(dx=3))

    def stage_f1r(*u):
        pass_on(u, pd(u), "pc", "pd", 14)

    gathered = set()

    def whole(u):
        if u not in gathered:
            gathered.add(u)
            U[u, "d", 0].wait_recv()
            if u in DIRECT_GATHER:
                U[u, "c", 0].wait_recv()
                U[u, "c", 1].wait_recv()
            else:
                U[u, "d", 1].wait_recv()

    def stage_p(*u):
        whole(u)
        U[u, "p"] = send(buf(agb, u), pd(u), *usem(u, 8), dev(dy=2))

    def stage_e(*u):
        kind = u[0]
        whole(u)
        if kind == 0:
            ready(3)
        n = len(sib_sends)
        if n >= SS:
            sib_sends[n - SS].wait_send()
            waited.append(id(sib_sends[n - SS]))
        m = size(u) // 2
        out = sibs.at[n % SS, 0:m]
        k = keep.at[slot_k.setdefault(u, free_k.pop(0)), 0:m]
        ag = buf(agb, u)
        lhs = jnp.concatenate([ag[rows((1 - c) * m, m)], ag[rows(c * m, m)]], axis=0)
        part = jnp.dot(lhs, wb[kind], preferred_element_type=F32)
        out[...] = part[:m].astype(BF)
        U[u, "e"] = send(out, buf(sibr, u, 2), *usem(u, 9), dev(dc=1))
        k[...] = part[m:]
        sib_sends.append(U[u, "e"])

    def stage_f(*u):
        kind, chunk = u
        U[u, "e"].wait_recv()
        m = size(u) // 2
        k, got = keep.at[slot_k[u], 0:m], buf(sibr, u, 2)
        relayed = kind in RELAY_Z and chunk in (1, 2)
        if relayed:
            U[kind, chunk, "zr"].wait_recv()
        for n in range(m // B):
            r = slice(n * B, n * B + B)
            total = k[r] + got[r].astype(F32)
            if relayed and n // 2 == chunk - 1:
                total = total + zr[kind, 2, r].astype(F32)
            if chunk in (0, 4):
                h = yh if chunk == 0 else 1 - yh
                s0[kind, rows(h * 64 + n * B, B)] = total
            else:
                got[r] = total.astype(BF)
        free_k.append(slot_k[u])
        if kind in RELAY_Z and chunk == 3:
            for i, d in ((1, 1), (2, 3)):
                r = slice(i * 64 - 64, i * 64)
                U[kind, i, "zr"] = send(
                    got.at[r], zr.at[kind, 2, r], *usem((kind, i), 11), dev(dz=d)
                )
        elif chunk not in (0, 4):
            U[kind, chunk, "z"] = send(
                got, zr.at[kind, chunk - 1], *usem(u, 10),
                dev(dz=OFFSET[chunk]),
            )

    z_done = set()

    def stage_g(kind, chunk):
        parts = (1, 2) if kind in RELAY_Z else (1, 2, 3)
        if kind not in z_done:
            z_done.add(kind)
            for i in parts:
                U[kind, i, "z"].wait_recv()

        def total(blk):
            r = rows(blk * B, B)
            t = s0[kind, r]
            for i in parts:
                t = t + zr[kind, i - 1, r].astype(F32)
            return t

        for d in (1,) if chunk == 0 else (2, 3):
            ys[kind, d - 1] = total(lax.rem(y + SHIFT[d], 4)).astype(BF)
            U[kind, d, "y"] = send(
                ys.at[kind, d - 1], yr.at[kind, d - 1], fsend.at[kind, d - 1],
                frecv.at[kind, d - 1], dev(dy=SHIFT[d]),
            )
        if chunk == 0:
            s0[kind, rows(y * B, B)] = total(y)

    def stage_h(kind):
        t = s0[kind, rows(y * B, B)]
        for d in (3, 2, 1):
            U[kind, d, "y"].wait_recv()
            t = t + yr[kind, d - 1].astype(F32)
        (lo_ref, tg_ref)[kind][...] = t.astype(BF)

    count = [0, 0]

    def lead(a, b):
        return lax.dot_general(a, b, (((0,), (0,)), ((), ())), preferred_element_type=F32)

    def stage_sg(part):
        at = slice(part * H, part * H + H)
        t = None
        for j in range(5):
            whole((0, j))
            group(1, j)
        for j in range(4):
            right = tokens(1, j, lanes=at)
            if j == 0:
                right = jnp.concatenate([right, tokens(1, 4, lanes=at)], axis=0)
            p = lead(agb[j], right)
            t = p if t is None else t + p
        sg_ref[:, at] = t.astype(BF)

    def first_grad(chunk, side, src):
        p = lead(tokens(0, chunk, side == 1, half), src[...])
        if count[side]:
            p = p + facc[side]
        count[side] += 1
        if count[side] < 5:
            facc[side] = p
            return
        fg_ref[:, rows((1 - yh if side else yh) * H, H)] = p.astype(BF)

    def stage_fo(chunk):
        whole((1, chunk))
        first_grad(chunk, 0, buf(agb, (1, chunk)))

    def stage_fp(chunk):
        u = (1, chunk)
        if chunk in F1:
            U[u, "pd", 0].wait_recv()
            if u in DIRECT_GATHER:
                U[u, "pc", 0].wait_recv()
                U[u, "pc", 1].wait_recv()
            else:
                U[u, "pd", 1].wait_recv()
        else:
            U[u, "p"].wait_recv()
        first_grad(chunk, 1, pd(u))

    def stage_t1():
        ready(3)
        wa[1] = wb[0].T

    def stage_t2():
        ready(2)
        wb[1] = wa[0].T

    steps = dict(
        gy=gather_y, gz=gather_z0, gz1=gather_z1, gz2=gather_z2,
        gr=gather_relay, gl=gather_last, t1=stage_t1,
        t2=stage_t2, a=stage_a, b=stage_b, c=stage_c, d=stage_d, p=stage_p, e=stage_e,
        f=stage_f, g=stage_g, h=stage_h, sg=stage_sg, fo=stage_fo, fp=stage_fp,
        f1s=stage_f1s, f1r=stage_f1r,
    )
    for name, *args in SCHEDULE:
        steps[name](*args)
    for cp in pending:
        if id(cp) not in waited:
            cp.wait_send()


def widen(lo_in, tg_in, fg_in, sg_in, lo_ref, tg_ref, fg_ref, sg_ref, wide, sem):
    copies = []
    size = H // 4
    for i in range(4):
        for a, (src, dst) in enumerate(((fg_in, fg_ref), (sg_in, sg_ref))):
            r = slice(i * size, i * size + size)
            wide[a, r] = src[r].astype(F32)
            cp = pltpu.make_async_copy(wide.at[a, r], dst.at[r], sem.at[a, i])
            cp.start()
            copies.append(cp)
    lo_ref[...] = lo_in[...]
    tg_ref[...] = tg_in[...]
    for cp in copies:
        cp.wait()


def local(tokens, first_weight, second_weight, upstream):
    vm = pl.BlockSpec(memory_space=pltpu.VMEM)
    hbm = pl.BlockSpec(memory_space=pl.ANY)
    dma = pltpu.SemaphoreType.DMA
    lo, tg, fg, sg = pl.pallas_call(
        kernel,
        out_shape=(
            pltpu.VMEM((B, W), BF),
            pltpu.VMEM((B, W), BF),
            pltpu.VMEM((H, W), BF),
            pltpu.VMEM((H, W), BF),
        ),
        in_specs=[hbm] * 4,
        out_specs=(vm,) * 4,
        scratch_shapes=[
            pltpu.VMEM((2, 4, C, W), BF),
            pltpu.VMEM((2, W, H), BF),
            pltpu.VMEM((2, H, W), BF),
            pltpu.VMEM((FS, C, H), F32),
            pltpu.VMEM((8, Q, H), BF),
            pltpu.VMEM((8, Q, H), BF),
            pltpu.VMEM((8, 2, Q, H), BF),
            pltpu.VMEM((8, 2, Q, H), BF),
            pltpu.VMEM((8, C, H), BF),
            pltpu.VMEM((4, Q, H), F32),
            pltpu.VMEM((4, C, H), BF),
            pltpu.VMEM((KS, 128, W), F32),
            pltpu.VMEM((SS, 128, W), BF),
            pltpu.VMEM((8, 128, W), BF),
            pltpu.VMEM((2, 3, 128, W), BF),
            pltpu.VMEM((2, 128, W), F32),
            pltpu.VMEM((2, 3, B, W), BF),
            pltpu.VMEM((2, 3, B, W), BF),
            pltpu.VMEM((2, H, H), F32),
            dma((4,)),
            dma((2, 20)), dma((2, 20)),
            dma((10, 16)), dma((10, 16)),
            dma((2, 3)), dma((2, 3)),
        ],
        compiler_params=pltpu.CompilerParams(
            collective_id=0, has_side_effects=True, vmem_limit_bytes=57 << 20
        ),
        cost_estimate=pl.CostEstimate(
            flops=6 * 2 * 1024 * W * H, bytes_accessed=16 << 20, transcendentals=0
        ),
        name="ffn",
    )(tokens, first_weight, second_weight, upstream)
    return pl.pallas_call(
        widen,
        out_shape=(
            jax.ShapeDtypeStruct((B, W), BF),
            jax.ShapeDtypeStruct((B, W), BF),
            jax.ShapeDtypeStruct((H, W), F32),
            jax.ShapeDtypeStruct((H, W), F32),
        ),
        in_specs=[vm] * 4,
        out_specs=(vm, vm, hbm, hbm),
        scratch_shapes=[pltpu.VMEM((2, H, W), F32), dma((2, 4))],
        compiler_params=pltpu.CompilerParams(vmem_limit_bytes=40 << 20),
        name="widen",
    )(lo, tg, fg, sg)


def solution(mesh):
    in_specs = (
        P(("col", "depth"), "row"),
        P("row", "col"),
        P("col", "row"),
        P(("col", "depth"), "row"),
    )
    out_specs = (
        P(("col", "depth"), "row"),
        P(("col", "depth"), "row"),
        P(("row", "depth"), "col"),
        P(("col", "depth"), "row"),
    )
    return jax.shard_map(local, mesh=mesh, in_specs=in_specs, out_specs=out_specs, check_vma=False)
```

```python
import math

import jax
import jax.numpy as jnp
from jax import lax
from jax.experimental import pallas as pl
from jax.experimental.pallas import tpu as pltpu
from jax.sharding import PartitionSpec as P

MESH = pl.DeviceIdType.MESH
BF = jnp.bfloat16
F32 = jnp.float32
SCALE = math.sqrt(2.0 / math.pi)

W = 1792
H = 896
C = 256
Q = 64
B = 32
OFFSET = (0, 1, 3, 2)
DIRECT_SUM = ((0, 0), (0, 4), (1, 0))
DIRECT_GATHER = ((1, 1), (1, 4))
FS, KS, SS = 4, 3, 3
RELAY_Z = (1,)
F1 = (1, 2, 4)

SCHEDULE = (
    ("gy", 0), ("gz", 0), ("gz1", 0), ("gy", 1), ("a", 0, 0), ("gz2", 0), ("a", 0, 4),
    ("t1",), ("gz", 1), ("gz1", 1), ("c", 0, 0), ("a", 1, 0), ("gz2", 1), ("gr", 0, 1),
    ("c", 0, 4), ("a", 1, 4), ("gr", 0, 2), ("a", 0, 1), ("c", 1, 0), ("a", 0, 2),
    ("b", 0, 1), ("b", 0, 2), ("gr", 1, 1), ("t2",), ("d", 1, 0), ("c", 0, 1), ("gr", 1, 2),
    ("gl", 0), ("c", 0, 2), ("a", 0, 3), ("e", 1, 0), ("p", 1, 0), ("d", 0, 1), ("gl", 1),
    ("d", 0, 2), ("b", 0, 3), ("a", 1, 3), ("a", 1, 2), ("e", 0, 1), ("d", 0, 4), ("c", 0, 3),
    ("e", 0, 2), ("f", 0, 1), ("b", 1, 3), ("f", 1, 0), ("f", 0, 2), ("d", 0, 3), ("b", 1, 2),
    ("a", 1, 1), ("fo", 0), ("e", 0, 4), ("c", 1, 3), ("e", 0, 3), ("b", 1, 1), ("f", 0, 3),
    ("d", 1, 3), ("c", 1, 2), ("c", 1, 1), ("e", 1, 3), ("p", 1, 3), ("f", 1, 3), ("fo", 3),
    ("d", 1, 2), ("b", 1, 4), ("e", 1, 1), ("e", 1, 2), ("f1s", 1, 2), ("fo", 1), ("f", 1, 1),
    ("f", 1, 2), ("d", 0, 0), ("f", 0, 4), ("c", 1, 4), ("fp", 0), ("e", 0, 0), ("fp", 3),
    ("f1s", 1, 4), ("f", 0, 0), ("g", 0, 4), ("sg", 0), ("g", 0, 0), ("f1s", 1, 1),
    ("e", 1, 4), ("fo", 4), ("f1r", 1, 2), ("fp", 4), ("f", 1, 4), ("g", 1, 4), ("fo", 2),
    ("h", 0), ("g", 1, 0), ("sg", 1), ("fp", 1), ("fp", 2), ("h", 1),
)


def gelu_and_slope(h):
    inner = SCALE * (h + 0.044715 * h * h * h)
    t = jnp.tanh(inner)
    value = 0.5 * h * (1.0 + t)
    slope = 0.5 * (1.0 + t) + 0.5 * h * (1.0 - t * t) * SCALE * (
        1.0 + 3.0 * 0.044715 * h * h
    )
    return value, slope


def kernel(
    tok_ref, w1_ref, w2_ref, up_ref,
    lo_ref, tg_ref, fg_ref, sg_ref,
    xs, wa, wb, hp, rs1s, rs1r, rs2s, rs2r, agb, slope, pdelta,
    keep, sibs, sibr, zr, s0, ys, yr, facc,
    lsem, gsend, grecv, usend, urecv, fsend, frecv,
):
    x = lax.axis_index("row")
    col = lax.axis_index("col")
    yh = lax.axis_index("depth")
    z, yl, c = col // 4, (col // 2) % 2, col % 2
    y = yh * 2 + yl

    def dev(dx=0, dy=0, dz=0, dc=0):
        xx, yy = lax.rem(x + dx, 4), lax.rem(y + dy, 4)
        zz, cc = lax.rem(z + dz, 4), lax.rem(c + dc, 2)
        return (xx, zz * 4 + lax.rem(yy, 2) * 2 + cc, yy // 2)

    pending, waited = [], []

    def send(src, dst, ss, rs, to):
        cp = pltpu.make_async_remote_copy(
            src_ref=src, dst_ref=dst, send_sem=ss, recv_sem=rs,
            device_id=to, device_id_type=MESH,
        )
        cp.start()
        pending.append(cp)
        return cp

    def rows(start, size):
        return pl.ds(pl.multiple_of(start, size), size)

    half = rows(yh * H, H)
    in_copies = [
        pltpu.make_async_copy(tok_ref, xs.at[0, z, rows(c * 128 + y * B, B)], lsem.at[0]),
        pltpu.make_async_copy(up_ref, xs.at[1, z, rows(c * 128 + y * B, B)], lsem.at[1]),
        pltpu.make_async_copy(w1_ref.at[:, half], wa.at[0], lsem.at[2]),
        pltpu.make_async_copy(w2_ref.at[half, :], wb.at[0], lsem.at[3]),
    ]
    for cp in in_copies:
        cp.start()
    loaded = set()

    def ready(i):
        if i not in loaded:
            loaded.add(i)
            in_copies[i].wait()

    barrier = pltpu.get_barrier_semaphore()
    peers = [dev(dc=1), dev(dx=1), dev(dx=2), dev(dx=3), dev(dy=1), dev(dy=2), dev(dy=3),
             dev(dz=1), dev(dz=2), dev(dz=3)]
    for p in peers:
        pl.semaphore_signal(barrier, inc=1, device_id=p, device_id_type=MESH)
    pl.semaphore_wait(barrier, len(peers))

    G = {}

    def gsem(k, i):
        return gsend.at[k, i], grecv.at[k, i]

    SHIFT = (0, 1 + 2 * yl, 2, 3 - 2 * yl)

    def gather_y(k):
        ready(k)
        blk = xs.at[k, z, rows(c * 128 + y * B, B)]
        for d in (1, 3, 2):
            G[k, "y", d] = send(blk, blk, *gsem(k, d - 1), dev(dy=SHIFT[d]))

    def forward(k, d):
        blk = xs.at[k, z, rows(c * 128 + lax.rem(y + SHIFT[d], 4) * B, B)]
        G[k, "s0", d] = send(blk, blk, *gsem(k, 3 + d), dev(dc=1))
        G[k, "z", 1, d] = send(blk, blk, *gsem(k, 7 + d), dev(dz=1))
        G[k, "z", 3, d] = send(blk, blk, *gsem(k, 11 + d), dev(dz=3))

    def gather_z0(k):
        forward(k, 0)

    def gather_z1(k):
        G[k, "y", 1].wait_recv()
        forward(k, 1)

    def gather_z2(k):
        for d in (3, 2):
            G[k, "y", d].wait_recv()
            forward(k, d)

    def gather_relay(k, chunk):
        zz = lax.rem(z + OFFSET[chunk], 4)
        for d in range(4):
            G[k, "z", 3 if chunk == 1 else 1, d].wait_recv()
        if chunk == 1:
            part = xs.at[k, zz, rows(c * 128 + 64, 64)]
            G[k, "r", 1] = send(part, part, *gsem(k, 15), dev(dz=3))
        else:
            part = xs.at[k, zz, rows(c * 128, 64)]
            G[k, "r", 2] = send(part, part, *gsem(k, 16), dev(dz=1))
        grp = xs.at[k, zz, rows(c * 128, 128)]
        G[k, "s", chunk] = send(grp, grp, *gsem(k, 16 + chunk), dev(dc=1))

    def gather_last(k):
        G[k, "r", 1].wait_recv()
        G[k, "r", 2].wait_recv()
        grp = xs.at[k, lax.rem(z + 2, 4), rows(c * 128, 128)]
        G[k, "s", 3] = send(grp, grp, *gsem(k, 19), dev(dc=1))

    grouped = set()

    def group(k, chunk):
        if (k, chunk) not in grouped:
            grouped.add((k, chunk))
            if chunk in (0, 4):
                for d in ((0, 1) if chunk == 0 else (3, 2)):
                    G[k, "s0", d].wait_recv()
            else:
                G[k, "s", chunk].wait_recv()

    U = {}
    free_f, free_k, sib_sends = list(range(FS)), list(range(KS)), []
    slot_f, slot_k = {}, {}

    def usem(u, i):
        n = u[0] * 5 + u[1]
        return usend.at[n, i], urecv.at[n, i]

    def size(u):
        return C // 2 if u[1] in (0, 4) else C

    def buf(ref, u, part=1, lead=()):
        m = size(u) // part
        start = m if u[1] == 4 else 0
        return ref.at[(u[0] * 4 + u[1] % 4,) + lead + (slice(start, start + m),)]

    def pd(u):
        return buf(pdelta, (0, u[1]))

    def tokens(k, chunk, other=False, lanes=slice(None)):
        if chunk in (0, 4):
            h = yh if (chunk == 0) != other else 1 - yh
            return jnp.concatenate(
                [xs[k, z, rows(cc * 128 + h * 64, 64), lanes] for cc in (0, 1)], axis=0
            )
        return xs[k, lax.rem(z + OFFSET[chunk], 4), :, lanes]

    def stage_a(*u):
        kind, chunk = u
        group(kind, chunk)
        if kind == 0:
            ready(2)
        q = size(u) // 4
        e = q // 2
        f = hp.at[slot_f.setdefault(u, free_f.pop(0)), 0 : size(u)]
        f[...] = jnp.dot(tokens(kind, chunk), wa[kind], preferred_element_type=F32)
        away, into = buf(rs1s, u, 4), buf(rs1r, u, 4)
        away[...] = f[rows(lax.rem(x + 2, 4) * q, q)].astype(BF)
        if u in DIRECT_SUM:
            U[u, "a", 0] = send(away, into, *usem(u, 0), dev(dx=2))
            for i, d in enumerate((1, 3)):
                out, into = buf(rs2s, u, 4, (i,)), buf(rs2r, u, 4, (i,))
                out[...] = f[rows(lax.rem(x + d, 4) * q, q)].astype(BF)
                U[u, "b", i] = send(out, into, *usem(u, 2 + i), dev(dx=d))
            return
        U[u, "a", 0] = send(away.at[0:e], into.at[0:e], *usem(u, 0), dev(dx=1))
        U[u, "a", 1] = send(away.at[e:q], into.at[e:q], *usem(u, 1), dev(dx=3))

    def stage_b(*u):
        q = size(u) // 4
        e = q // 2
        f, got = hp.at[slot_f[u], 0 : size(u)], buf(rs1r, u, 4)
        for i, d in enumerate((1, 3)):
            out, into = buf(rs2s, u, 4, (i,)), buf(rs2r, u, 4, (i,))
            start = lax.rem(x + d, 4) * q
            r, o = (slice(0, e), slice(e, q))[:: 1 - 2 * i]
            U[u, "a", i].wait_recv()
            out[r] = (f[rows(start + i * e, e)] + got[r].astype(F32)).astype(BF)
            out[o] = f[rows(start + e - i * e, e)].astype(BF)
            U[u, "b", i] = send(out, into, *usem(u, 2 + i), dev(dx=d))

    def stage_c(*u):
        kind, chunk = u
        q = size(u) // 4
        f, ag = hp.at[slot_f[u], 0 : size(u)], buf(agb, u)
        right, left = buf(rs2r, u, 4, (0,)), buf(rs2r, u, 4, (1,))
        sl_ref = buf(slope, (0, chunk), 4)
        U[u, "b", 0].wait_recv()
        U[u, "b", 1].wait_recv()
        if u in DIRECT_SUM:
            U[u, "a", 0].wait_recv()
        for n in range(0, q, 32):
            r = slice(n, n + 32)
            h = f[rows(x * q + n, 32)] + right[r].astype(F32) + left[r].astype(F32)
            if u in DIRECT_SUM:
                h = h + buf(rs1r, u, 4)[r].astype(F32)
            if kind == 0:
                value, sl = gelu_and_slope(h)
                sl_ref[r] = sl
            else:
                value = h * sl_ref[r]
            ag[rows(x * q + n, 32)] = value.astype(BF)
        free_f.append(slot_f[u])
        mine = ag.at[rows(x * q, q)]
        if kind == 1 and chunk in F1:
            U[u, "p"] = send(mine, pd(u).at[rows(x * q, q)], *usem(u, 8), dev(dy=2))
        if u in DIRECT_GATHER:
            U[u, "d", 0] = send(mine, mine, *usem(u, 6), dev(dx=2))
        U[u, "c", 0] = send(mine, mine, *usem(u, 4), dev(dx=1))
        U[u, "c", 1] = send(mine, mine, *usem(u, 5), dev(dx=3))

    def pass_on(u, ref, first, then, sem):
        q = size(u) // 4
        e = q // 2
        U[u, first, 0].wait_recv()
        part = ref.at[rows(lax.rem(x + 3, 4) * q, e)]
        U[u, then, 0] = send(part, part, *usem(u, sem), dev(dx=1))
        U[u, first, 1].wait_recv()
        part = ref.at[rows(lax.rem(x + 1, 4) * q + e, e)]
        U[u, then, 1] = send(part, part, *usem(u, sem + 1), dev(dx=3))

    def stage_d(*u):
        pass_on(u, buf(agb, u), "c", "d", 6)

    def stage_f1s(*u):
        q = size(u) // 4
        part = pd(u).at[rows(x * q, q)]
        U[u, "p"].wait_recv()
        if u in DIRECT_GATHER:
            U[u, "pd", 0] = send(part, part, *usem(u, 14), dev(dx=2))
        U[u, "pc", 0] = send(part, part, *usem(u, 12), dev(dx=1))
        U[u, "pc", 1] = send(part, part, *usem(u, 13), dev(dx=3))

    def stage_f1r(*u):
        pass_on(u, pd(u), "pc", "pd", 14)

    gathered = set()

    def whole(u):
        if u not in gathered:
            gathered.add(u)
            U[u, "d", 0].wait_recv()
            if u in DIRECT_GATHER:
                U[u, "c", 0].wait_recv()
                U[u, "c", 1].wait_recv()
            else:
                U[u, "d", 1].wait_recv()

    def stage_p(*u):
        whole(u)
        U[u, "p"] = send(buf(agb, u), pd(u), *usem(u, 8), dev(dy=2))

    def stage_e(*u):
        kind = u[0]
        whole(u)
        if kind == 0:
            ready(3)
        n = len(sib_sends)
        if n >= SS:
            sib_sends[n - SS].wait_send()
            waited.append(id(sib_sends[n - SS]))
        m = size(u) // 2
        out = sibs.at[n % SS, 0:m]
        k = keep.at[slot_k.setdefault(u, free_k.pop(0)), 0:m]
        ag = buf(agb, u)
        lhs = jnp.concatenate([ag[rows((1 - c) * m, m)], ag[rows(c * m, m)]], axis=0)
        part = jnp.dot(lhs, wb[kind], preferred_element_type=F32)
        out[...] = part[:m].astype(BF)
        U[u, "e"] = send(out, buf(sibr, u, 2), *usem(u, 9), dev(dc=1))
        k[...] = part[m:]
        sib_sends.append(U[u, "e"])

    def stage_f(*u):
        kind, chunk = u
        U[u, "e"].wait_recv()
        m = size(u) // 2
        k, got = keep.at[slot_k[u], 0:m], buf(sibr, u, 2)
        relayed = kind in RELAY_Z and chunk in (1, 2)
        if relayed:
            U[kind, chunk, "zr"].wait_recv()
        for n in range(m // B):
            r = slice(n * B, n * B + B)
            total = k[r] + got[r].astype(F32)
            if relayed and n // 2 == chunk - 1:
                total = total + zr[kind, 2, r].astype(F32)
            if chunk in (0, 4):
                h = yh if chunk == 0 else 1 - yh
                s0[kind, rows(h * 64 + n * B, B)] = total
            else:
                got[r] = total.astype(BF)
        free_k.append(slot_k[u])
        if kind in RELAY_Z and chunk == 3:
            for i, d in ((1, 1), (2, 3)):
                r = slice(i * 64 - 64, i * 64)
                U[kind, i, "zr"] = send(
                    got.at[r], zr.at[kind, 2, r], *usem((kind, i), 11), dev(dz=d)
                )
        elif chunk not in (0, 4):
            U[kind, chunk, "z"] = send(
                got, zr.at[kind, chunk - 1], *usem(u, 10),
                dev(dz=OFFSET[chunk]),
            )

    z_done = set()

    def stage_g(kind, chunk):
        parts = (1, 2) if kind in RELAY_Z else (1, 2, 3)
        if kind not in z_done:
            z_done.add(kind)
            for i in parts:
                U[kind, i, "z"].wait_recv()

        def total(blk):
            r = rows(blk * B, B)
            t = s0[kind, r]
            for i in parts:
                t = t + zr[kind, i - 1, r].astype(F32)
            return t

        for d in (1,) if chunk == 0 else (2, 3):
            ys[kind, d - 1] = total(lax.rem(y + SHIFT[d], 4)).astype(BF)
            U[kind, d, "y"] = send(
                ys.at[kind, d - 1], yr.at[kind, d - 1], fsend.at[kind, d - 1],
                frecv.at[kind, d - 1], dev(dy=SHIFT[d]),
            )
        if chunk == 0:
            s0[kind, rows(y * B, B)] = total(y)

    def stage_h(kind):
        t = s0[kind, rows(y * B, B)]
        for d in (3, 2, 1):
            U[kind, d, "y"].wait_recv()
            t = t + yr[kind, d - 1].astype(F32)
        (lo_ref, tg_ref)[kind][...] = t.astype(BF)

    count = [0, 0]

    def lead(a, b):
        return lax.dot_general(a, b, (((0,), (0,)), ((), ())), preferred_element_type=F32)

    def stage_sg(part):
        at = slice(part * H, part * H + H)
        t = None
        for j in range(5):
            whole((0, j))
            group(1, j)
        for j in range(4):
            right = tokens(1, j, lanes=at)
            if j == 0:
                right = jnp.concatenate([right, tokens(1, 4, lanes=at)], axis=0)
            p = lead(agb[j], right)
            t = p if t is None else t + p
        sg_ref[:, at] = t.astype(BF)

    def first_grad(chunk, side, src):
        p = lead(tokens(0, chunk, side == 1, half), src[...])
        if count[side]:
            p = p + facc[side]
        count[side] += 1
        if count[side] < 5:
            facc[side] = p
            return
        fg_ref[:, rows((1 - yh if side else yh) * H, H)] = p.astype(BF)

    def stage_fo(chunk):
        whole((1, chunk))
        first_grad(chunk, 0, buf(agb, (1, chunk)))

    def stage_fp(chunk):
        u = (1, chunk)
        if chunk in F1:
            U[u, "pd", 0].wait_recv()
            if u in DIRECT_GATHER:
                U[u, "pc", 0].wait_recv()
                U[u, "pc", 1].wait_recv()
            else:
                U[u, "pd", 1].wait_recv()
        else:
            U[u, "p"].wait_recv()
        first_grad(chunk, 1, pd(u))

    def stage_t1():
        ready(3)
        wa[1] = wb[0].T

    def stage_t2():
        ready(2)
        wb[1] = wa[0].T

    steps = dict(
        gy=gather_y, gz=gather_z0, gz1=gather_z1, gz2=gather_z2,
        gr=gather_relay, gl=gather_last, t1=stage_t1,
        t2=stage_t2, a=stage_a, b=stage_b, c=stage_c, d=stage_d, p=stage_p, e=stage_e,
        f=stage_f, g=stage_g, h=stage_h, sg=stage_sg, fo=stage_fo, fp=stage_fp,
        f1s=stage_f1s, f1r=stage_f1r,
    )
    for name, *args in SCHEDULE:
        steps[name](*args)
    for cp in pending:
        if id(cp) not in waited:
            cp.wait_send()


def widen(lo_in, tg_in, fg_in, sg_in, lo_ref, tg_ref, fg_ref, sg_ref, wide, sem):
    copies = []
    size = H // 4
    for i in range(4):
        for a, (src, dst) in enumerate(((fg_in, fg_ref), (sg_in, sg_ref))):
            r = slice(i * size, i * size + size)
            wide[a, r] = src[r].astype(F32)
            cp = pltpu.make_async_copy(wide.at[a, r], dst.at[r], sem.at[a, i])
            cp.start()
            copies.append(cp)
    lo_ref[...] = lo_in[...]
    tg_ref[...] = tg_in[...]
    for cp in copies:
        cp.wait()


def local(tokens, first_weight, second_weight, upstream):
    vm = pl.BlockSpec(memory_space=pltpu.VMEM)
    hbm = pl.BlockSpec(memory_space=pl.ANY)
    dma = pltpu.SemaphoreType.DMA
    lo, tg, fg, sg = pl.pallas_call(
        kernel,
        out_shape=(
            pltpu.VMEM((B, W), BF),
            pltpu.VMEM((B, W), BF),
            pltpu.VMEM((H, W), BF),
            pltpu.VMEM((H, W), BF),
        ),
        in_specs=[hbm] * 4,
        out_specs=(vm,) * 4,
        scratch_shapes=[
            pltpu.VMEM((2, 4, C, W), BF),
            pltpu.VMEM((2, W, H), BF),
            pltpu.VMEM((2, H, W), BF),
            pltpu.VMEM((FS, C, H), F32),
            pltpu.VMEM((8, Q, H), BF),
            pltpu.VMEM((8, Q, H), BF),
            pltpu.VMEM((8, 2, Q, H), BF),
            pltpu.VMEM((8, 2, Q, H), BF),
            pltpu.VMEM((8, C, H), BF),
            pltpu.VMEM((4, Q, H), F32),
            pltpu.VMEM((4, C, H), BF),
            pltpu.VMEM((KS, 128, W), F32),
            pltpu.VMEM((SS, 128, W), BF),
            pltpu.VMEM((8, 128, W), BF),
            pltpu.VMEM((2, 3, 128, W), BF),
            pltpu.VMEM((2, 128, W), F32),
            pltpu.VMEM((2, 3, B, W), BF),
            pltpu.VMEM((2, 3, B, W), BF),
            pltpu.VMEM((2, H, H), F32),
            dma((4,)),
            dma((2, 20)), dma((2, 20)),
            dma((10, 16)), dma((10, 16)),
            dma((2, 3)), dma((2, 3)),
        ],
        compiler_params=pltpu.CompilerParams(
            collective_id=0, has_side_effects=True, vmem_limit_bytes=57 << 20
        ),
        cost_estimate=pl.CostEstimate(
            flops=6 * 2 * 1024 * W * H, bytes_accessed=16 << 20, transcendentals=0
        ),
        name="ffn",
    )(tokens, first_weight, second_weight, upstream)
    return pl.pallas_call(
        widen,
        out_shape=(
            jax.ShapeDtypeStruct((B, W), BF),
            jax.ShapeDtypeStruct((B, W), BF),
            jax.ShapeDtypeStruct((H, W), F32),
            jax.ShapeDtypeStruct((H, W), F32),
        ),
        in_specs=[vm] * 4,
        out_specs=(vm, vm, hbm, hbm),
        scratch_shapes=[pltpu.VMEM((2, H, W), F32), dma((2, 4))],
        compiler_params=pltpu.CompilerParams(vmem_limit_bytes=40 << 20),
        name="widen",
    )(lo, tg, fg, sg)


def solution(mesh):
    in_specs = (
        P(("col", "depth"), "row"),
        P("row", "col"),
        P("col", "row"),
        P(("col", "depth"), "row"),
    )
    out_specs = (
        P(("col", "depth"), "row"),
        P(("col", "depth"), "row"),
        P(("row", "depth"), "col"),
        P(("col", "depth"), "row"),
    )
    return jax.shard_map(local, mesh=mesh, in_specs=in_specs, out_specs=out_specs, check_vma=False)
```
